512 devices in a mesh: slab: 128 (over y, z, core), sub: 4 (over x).
Axes of the slice: x: 4, y: 8, z: 8, core: 2. Of those that a mesh axis runs over, the one named last changes fastest.
Arguments:
- leaves: bfloat16 [131072, 512], P(('slab', 'sub')), may hold values from -6 to 6
- m2l_ops: bfloat16 [16, 512, 512], P('sub'), may hold values from -0.09375 to 0.09375
- send_index: int32 [128, 128, 8], P('slab'), may hold values from 0 to 127
- pair_target: int32 [128, 16, 128], P('slab', 'sub'), may hold values from 0 to 127, each once within a row
- pair_source: int32 [128, 16, 128], P('slab', 'sub'), may hold values from 0 to 1151
- pair_count: int32 [128, 16], P('slab', 'sub'), may hold values from 25 to 128, as said below
Outputs:
- parent_multipoles: bfloat16 [16384, 512], P(('slab', 'sub'))
- local_expansions: float32 [16384, 512], P(('slab', 'sub'))
The draws below stay inside these ranges and needn't reach their ends.
Inputs may be any that keep to these rules, and one draw needn't show every extreme that they name: `pair_count`: in every segment at least one operator, has all 128 slots live.
All inputs are finite; a program needn't handle non-finite values.
Results may differ from the reference program's by a relative error of at most 0.014.
Values may be sent and summed in bfloat16 or wider, within the bound.
No kernel may reach another device: no remote copies, remote signals or barrier semaphores. Data moves between devices by JAX's collectives and lax.ppermute only.
A program may use at most 64 MiB of HBM per device.

```python
import math
import jax
import jax.numpy as jnp
from jax import lax

ORDER = 8
NODES = 512
OPS = 16
GHOST = 8
P_SEG = 128
CAP = 128
TABLE = 1152
PARENTS = 16384
LEAVES = 131072
N_SLAB = 128


def draw_pair_count(key, part):
    key = jax.random.fold_in(key, 11)
    first, second = jax.random.split(key)
    segments = PARENTS // P_SEG
    base = jax.random.randint(first, (segments, OPS), CAP // 5, CAP + 1)
    chosen = jax.random.randint(second, (segments, 1), 0, OPS)
    columns = jnp.arange(OPS, dtype=jnp.int32)[None, :]
    return jnp.where(columns == chosen, CAP, base).astype(jnp.int32)


def plant(entries, stream_key, smallest, largest):
    index_at = [jax.random.randint(jax.random.fold_in(stream_key, axis), (), 0, length) for axis, length in enumerate(entries.shape)]
    main_axis = entries.shape.index(max(entries.shape))
    beside = index_at[:main_axis] + [(index_at[main_axis] + 1) % entries.shape[main_axis]] + index_at[main_axis + 1:]
    return entries.at[tuple(index_at)].set(smallest).at[tuple(beside)].set(largest)


def block_levels(rng, dims, shards, least, largest):
    level, own = 1.0, jax.random.fold_in(rng, 6)
    for position, parts in shards:
        steps = jnp.exp(jax.random.uniform(jax.random.fold_in(own, position), (parts,), jnp.float32, least / len(shards), largest / len(shards)))
        level = level * jnp.repeat(steps, dims[position] // parts).reshape([-1 if axis == position else 1 for axis in range(len(dims))])
    return level


def normal_values(own_key, shape, spread, most, pieces=(), kind=jnp.bfloat16):
    values = spread * jax.random.normal(own_key, shape, jnp.float32)
    if pieces:
        values = values * block_levels(own_key, shape, pieces, -0.22, 0.18)
    return jnp.clip(values, -most, most).astype(kind)


def setup_inputs(seed: int = 0) -> dict:
    splits = jax.random.split(jax.random.key(seed), 7)
    leaves = normal_values(splits[0], (LEAVES, NODES), 0.5, 6.0, ((0, 512),))
    m2l_ops = normal_values(splits[1], (OPS, NODES, NODES), (NODES * OPS // 2) ** -0.5, 0.09375, ((0, 4),))
    send_index = plant(jax.random.randint(splits[2], (N_SLAB, N_SLAB, GHOST), 0, P_SEG), jax.random.fold_in(splits[2], 1), 0, P_SEG - 1).astype(jnp.int32)
    pair_target = jax.vmap(lambda own: jax.random.permutation(own, P_SEG))(jax.random.split(splits[3], N_SLAB * OPS)).reshape((N_SLAB, OPS, CAP)).astype(jnp.int32)
    pair_source = plant(jax.random.randint(splits[4], (N_SLAB, OPS, CAP), 0, TABLE), jax.random.fold_in(splits[4], 1), 0, TABLE - 1).astype(jnp.int32)
    pair_count = draw_pair_count(jax.random.fold_in(splits[6], 71), 0)
    return {"leaves": leaves, "m2l_ops": m2l_ops, "send_index": send_index, "pair_target": pair_target, "pair_source": pair_source, "pair_count": pair_count}


def one_side(order, side):
    counter = jnp.arange(order, dtype=jnp.float32)
    angles = (2.0 * counter + 1.0) * math.pi / (2.0 * order)
    nodes = jnp.cos(angles)
    degree = jnp.arange(1, order, dtype=jnp.float32)
    parent_poly = jnp.cos(degree[:, None] * angles[None, :])
    child_pts = (nodes + (2.0 * side - 1.0)) / 2.0
    child_poly = jnp.cos(degree[:, None] * jnp.arccos(child_pts)[None, :])
    summed = jnp.sum(parent_poly[:, :, None] * child_poly[:, None, :], axis=0)
    return 1.0 / order + (2.0 / order) * summed


def upward_matrix(order):
    sides = [one_side(order, 0), one_side(order, 1)]
    blocks = []
    for octant in range(8):
        first = sides[(octant >> 2) & 1]
        second = sides[(octant >> 1) & 1]
        third = sides[octant & 1]
        blocks.append(jnp.kron(first, jnp.kron(second, third)).T)
    return jnp.concatenate(blocks, axis=0).astype(jnp.bfloat16)


def reference(leaves, m2l_ops, send_index, pair_target, pair_source, pair_count):
    weights = upward_matrix(ORDER)
    parents = jnp.dot(leaves.reshape(PARENTS, 8 * NODES), weights, preferred_element_type=jnp.float32).astype(jnp.bfloat16)
    segments = parents.reshape(N_SLAB, P_SEG, NODES)
    owners = jnp.arange(N_SLAB, dtype=jnp.int32)
    slots = jnp.arange(CAP, dtype=jnp.int32)

    def per_segment(receiver):
        picks = send_index[:, receiver, :].astype(jnp.int32)
        ghosts = segments[owners[:, None], picks]
        table = jnp.concatenate([segments[receiver], ghosts.reshape(N_SLAB * GHOST, NODES)], axis=0).astype(jnp.float32)

        def per_operator(total, index):
            source = table[pair_source[receiver, index]]
            image = jnp.dot(source, m2l_ops[index].astype(jnp.float32).T, precision=lax.Precision.HIGHEST)
            live = (slots < pair_count[receiver, index]).astype(jnp.float32)
            added = jax.ops.segment_sum(image * live[:, None], pair_target[receiver, index], num_segments=P_SEG)
            return total + added, None

        start = jnp.zeros((P_SEG, NODES), jnp.float32)
        total, unused = lax.scan(per_operator, start, jnp.arange(OPS, dtype=jnp.int32))
        return total

    local = lax.map(per_segment, jnp.arange(N_SLAB, dtype=jnp.int32))
    return parents, local.reshape(PARENTS, NODES)
```

```python
import functools
import math

import jax
import jax.numpy as jnp
import numpy as np
from jax import lax
from jax.experimental import pallas as pl
from jax.experimental.pallas import tpu as pltpu
from jax.sharding import Mesh, PartitionSpec as P

ORDER = 8
NODES = 512
SEG = 128
GHOST = 8
TABLE = 1152
BASE = 32
CHIPS = 64
SUBS = 4
PEERS = 8
ROWS = 32
MSG = 48
EIGHTH = 64
LANES = 128
WIDTH = 384
PLAN_FLOPS = 1 << 34
VMEM = 60 << 20
SMALL_VMEM = 16 << 20
BF = jnp.bfloat16
F32 = jnp.float32


def one_side(side):
    counter = np.arange(ORDER, dtype=np.float32)
    angles = (np.float32(2.0) * counter + np.float32(1.0)) * np.float32(math.pi) / np.float32(2.0 * ORDER)
    nodes = np.cos(angles)
    degree = np.arange(1, ORDER, dtype=np.float32)
    parent_poly = np.cos(degree[:, None] * angles[None, :])
    child_pts = (nodes + np.float32(2.0 * side - 1.0)) / np.float32(2.0)
    child_poly = np.cos(degree[:, None] * np.arccos(child_pts)[None, :])
    summed = np.sum(parent_poly[:, :, None] * child_poly[:, None, :], axis=0)
    return (np.float32(1.0 / ORDER) + np.float32(2.0 / ORDER) * summed).astype(np.float32)


def upward_matrix():
    sides = [one_side(0), one_side(1)]
    blocks = []
    for octant in range(8):
        first = sides[octant >> 2 & 1]
        second = sides[octant >> 1 & 1]
        third = sides[octant & 1]
        blocks.append(np.kron(first, np.kron(second, third)).T)
    return np.stack(blocks).astype(BF)


def dot(a, b):
    return lax.dot_general(a, b, (((1,), (0,)), ((), ())), preferred_element_type=F32)


def dot_t(a, b):
    return lax.dot_general(a, b, (((1,), (1,)), ((), ())), preferred_element_type=F32)


def iota(shape, axis):
    return lax.broadcasted_iota(jnp.int32, shape, axis)


def onehot(flags):
    return jnp.where(flags, 1.0, 0.0).astype(BF)


def upward_kernel(
    count_hbm, leaves_hbm, target_hbm, source_hbm, send_hbm, weights_hbm, ops_hbm,
    parents_ref, msg_ref, own_ref, side_ref, across_ref,
    count_ref, leaves_ref, target_ref, source_ref, send_ref, w_ref, ops_ref, sems,
):
    sub, core = lax.axis_index("x"), lax.axis_index("c")
    pairs = ((count_hbm, count_ref), (target_hbm, target_ref), (source_hbm, source_ref), (send_hbm, send_ref), (leaves_hbm, leaves_ref))
    copies = [pltpu.make_async_copy(source, to, sems.at[i]) for i, (source, to) in enumerate(pairs)]
    copies += [pltpu.make_async_copy(ops_hbm.at[k], ops_ref.at[k], sems.at[5 + k]) for k in range(4)]
    copies += [pltpu.make_async_copy(weights_hbm.at[c], w_ref.at[c], sems.at[9 + c]) for c in range(8)]
    for copy in copies:
        copy.start()
    for copy in copies[:4]:
        copy.wait()
    slot = iota((1, SEG), 1)
    row = iota((8, SEG), 0)
    info = jnp.zeros((8, SEG), F32)
    for k in range(4):
        live = slot < count_ref[0:1, k : k + 1]
        target = jnp.where(live, target_ref[0, k : k + 1, :], -1)
        source = source_ref[0, k : k + 1, :]
        match = onehot(iota((SEG, SEG), 0) == target)
        high = jnp.where(live, (source >> 5) + 1, 0).astype(F32)
        low = jnp.where(live, source & (BASE - 1), 0).astype(F32)
        info = info + dot_t(jnp.where(row == k, high, jnp.where(row == 4 + k, low, 0.0)).astype(BF), match)
    tail = jnp.concatenate([send_ref[...].astype(F32), info], axis=0).astype(BF)
    for e in range(PEERS):
        msg_ref[e, ROWS:MSG, :] = tail
    to, at = iota((256, 256), 0), iota((256, 256), 1)
    sort = onehot(at == (to & 31) * 8 + (to >> 5))
    copies[4].wait()
    sorted_leaves = dot(sort, leaves_ref[...]).astype(BF)
    for copy in copies[5:9]:
        copy.wait()
    to, at = iota((4 * EIGHTH, 4 * LANES), 0), iota((4 * EIGHTH, 4 * LANES), 1)

    def columns(c, x):
        start = pl.multiple_of((2 * c + (x >> 1)) * LANES, LANES)
        tiles = jnp.concatenate([ops_ref[k, :, pl.ds(start, LANES)] for k in range(4)], axis=1)
        pick = onehot(at == (to >> 6) * LANES + (x & 1) * EIGHTH + (to & (EIGHTH - 1)))
        return dot_t(pick, tiles).astype(BF)

    beside = (sub + 3 + 2 * core) & 3
    across_ref[...] = columns(core, (sub + 2) & 3)
    side_ref[0] = columns(core, beside)
    side_ref[1] = columns(1 - core, beside)
    own_ref[...] = columns(core, sub)
    total = jnp.zeros((ROWS, NODES), F32)
    for c in range(8):
        copies[9 + c].wait()
        total = total + dot(sorted_leaves[c * ROWS : (c + 1) * ROWS, :], w_ref[c])
    parents = total.astype(BF)
    parents_ref[...] = parents
    wide = parents.astype(F32)
    lane = iota((ROWS, LANES), 1)
    for j in range(4):
        block = wide[:, j * LANES : (j + 1) * LANES]
        turned = pltpu.roll(block, EIGHTH, 1)
        msg_ref[2 * j, 0:ROWS, :] = jnp.where(lane < EIGHTH, block, turned).astype(BF)
        msg_ref[2 * j + 1, 0:ROWS, :] = jnp.where(lane < EIGHTH, turned, block).astype(BF)


def upward(leaves, target, source, count, send, weights, ops):
    vmem = pl.BlockSpec(memory_space=pltpu.VMEM)
    return pl.pallas_call(
        upward_kernel,
        out_shape=(jax.ShapeDtypeStruct((ROWS, NODES), BF), jax.ShapeDtypeStruct((PEERS, MSG, LANES), BF))
        + tuple(jax.ShapeDtypeStruct(shape + (4 * EIGHTH, NODES), BF) for shape in ((), (2,), ())),
        in_specs=[pl.BlockSpec(memory_space=pl.ANY)] * 7,
        out_specs=(vmem,) * 5,
        scratch_shapes=[
            pltpu.VMEM((1, 4), jnp.int32),
            pltpu.VMEM((256, NODES), BF),
            pltpu.VMEM((1, 4, SEG), jnp.int32),
            pltpu.VMEM((1, 4, SEG), jnp.int32),
            pltpu.VMEM((GHOST, SEG), jnp.int32),
            pltpu.VMEM((8, NODES, NODES), BF),
            pltpu.VMEM((4, NODES, NODES), BF),
            pltpu.SemaphoreType.DMA((17,)),
        ],
        compiler_params=pltpu.CompilerParams(vmem_limit_bytes=VMEM),
        cost_estimate=pl.CostEstimate(flops=2 * 256 * 512 * 512, bytes_accessed=5 << 20, transcendentals=0),
        name="upward",
    )(count, leaves, target, source, send, weights, ops)


def pick_kernel(got_ref, out_ref):
    parents = jnp.concatenate([got_ref[j, 0:ROWS, :] for j in range(PEERS)], axis=0)
    lane = iota((2 * SEG, LANES), 1)
    zero = jnp.zeros_like(parents)
    rhs = jnp.concatenate([jnp.where(lane < EIGHTH, parents, zero), jnp.where(lane < EIGHTH, zero, parents)], axis=0)
    send = jnp.concatenate([got_ref[0, ROWS : ROWS + 8, :].astype(F32), got_ref[4, ROWS : ROWS + 8, :].astype(F32) + SEG], axis=0)
    send = send.astype(jnp.int32)
    at = iota((16, 2 * SEG), 1)
    step = 16
    for first in range(0, CHIPS, step):
        blocks = []
        for d in range(first, first + step):
            halves = [onehot(send[:, 2 * d + h : 2 * d + h + 1] == at) for h in range(2)]
            blocks.append(jnp.concatenate(halves, axis=1))
        lhs = jnp.concatenate(blocks, axis=0)
        out_ref[first * 16 : (first + step) * 16, :] = dot(lhs, rhs).astype(BF)


def pick(got):
    vmem = pl.BlockSpec(memory_space=pltpu.VMEM)
    return pl.pallas_call(
        pick_kernel,
        out_shape=jax.ShapeDtypeStruct((CHIPS * 16, LANES), BF),
        in_specs=[vmem],
        out_specs=vmem,
        compiler_params=pltpu.CompilerParams(vmem_limit_bytes=SMALL_VMEM),
        cost_estimate=pl.CostEstimate(flops=PLAN_FLOPS, bytes_accessed=1 << 19, transcendentals=0),
        name="pick",
    )(got)


def plan_kernel(got_ref, early_ref, late_ref, out_ref):
    sub, core = lax.axis_index("x"), lax.axis_index("c")
    groups = (sub, sub + 1 + 2 * core, sub + 2, sub + 3 + 2 * core)
    for q in range(2):
        for d in range(SUBS):
            info = got_ref[q * 4 + (groups[d] & 3), ROWS + 8 : MSG, :].astype(F32)
            source = ((info[0:4, :] - 1.0) * BASE + info[4:8, :]).astype(jnp.int32)
            ghost = source - SEG
            at = q * 16 + d * 4
            out_ref[at : at + 4, :] = jnp.where(source < SEG, jnp.where(source < 0, -1, source + 256), ghost & 255)
            out_ref[32 + at : 36 + at, :] = jnp.where(source < SEG, 0, ghost >> 8)


def plan(got, early, late):
    vmem = pl.BlockSpec(memory_space=pltpu.VMEM)
    return pl.pallas_call(
        plan_kernel,
        out_shape=jax.ShapeDtypeStruct((64, SEG), jnp.int32),
        in_specs=[vmem] + [pl.BlockSpec(memory_space=pl.ANY)] * 2,
        out_specs=vmem,
        compiler_params=pltpu.CompilerParams(vmem_limit_bytes=SMALL_VMEM),
        cost_estimate=pl.CostEstimate(flops=PLAN_FLOPS, bytes_accessed=5 << 20, transcendentals=0),
        name="plan",
    )(got, early, late)


def local_kernel(got_ref, ghosts_ref, plan_ref, m0_hbm, m1_hbm, m2_hbm, m3_hbm, out_ref, m_ref, rows_ref, rhs_ref, x_ref, sems):
    sources = (m0_hbm, m1_hbm.at[0], m2_hbm, m3_hbm)
    copies = [pltpu.make_async_copy(m, m_ref.at[d], sems.at[d]) for d, m in enumerate(sources)]
    for copy in copies:
        copy.start()
    row = iota((WIDTH, SEG), 0)
    for q in range(2):
        for k in range(16):
            at = q * 16 + k
            rows_ref[q, :, k * SEG : (k + 1) * SEG] = onehot(plan_ref[at : at + 1, :] == row)
    for q in range(2):
        own = jnp.concatenate([got_ref[q * 4 + j, 0:ROWS, 0:EIGHTH] for j in range(4)], axis=0).astype(F32).T
        rhs_ref[q, 0:EIGHTH, 256:WIDTH] = own.astype(BF)
        rhs_ref[q, EIGHTH:256, 256:WIDTH] = jnp.zeros((256 - EIGHTH, SEG), BF)
    for b in range(4):
        block = ghosts_ref[b * 256 : (b + 1) * 256, :].astype(F32).T.astype(BF)
        rhs_ref[0, b * EIGHTH : (b + 1) * EIGHTH, 0:256] = block[0:EIGHTH, :]
        rhs_ref[1, b * EIGHTH : (b + 1) * EIGHTH, 0:256] = block[EIGHTH:LANES, :]
    for q in range(2):
        for k in range(0, 16, 2):
            both = dot(rhs_ref[q], rows_ref[q, :, k * SEG : (k + 2) * SEG])
            for i in range(k, k + 2):
                at = 32 + q * 16 + i
                block = plan_ref[at : at + 1, :]
                part = both[:, (i - k) * SEG : (i - k + 1) * SEG]
                kept = jnp.where(block == 0, part[0:EIGHTH, :], 0.0)
                for b in range(1, 4):
                    kept = jnp.where(block == b, part[b * EIGHTH : (b + 1) * EIGHTH, :], kept)
                x_ref[i * EIGHTH : (i + 1) * EIGHTH, q * SEG : (q + 1) * SEG] = kept.astype(BF)
    for copy in copies:
        copy.wait()
    total = lax.dot_general(x_ref[...], m_ref[...].reshape(1024, NODES), (((0,), (0,)), ((), ())), preferred_element_type=F32)
    out_ref[...] = total.astype(BF)


def local_sums(got, ghosts, columns, ops):
    vmem, anywhere = pl.BlockSpec(memory_space=pltpu.VMEM), pl.BlockSpec(memory_space=pl.ANY)
    return pl.pallas_call(
        local_kernel,
        out_shape=jax.ShapeDtypeStruct((2 * SEG, NODES), BF),
        in_specs=[vmem] * 3 + [anywhere] * 4,
        out_specs=vmem,
        scratch_shapes=[
            pltpu.VMEM((SUBS, 256, NODES), BF),
            pltpu.VMEM((2, WIDTH, 16 * SEG), BF),
            pltpu.VMEM((2, 256, WIDTH), BF),
            pltpu.VMEM((1024, 2 * SEG), BF),
            pltpu.SemaphoreType.DMA((4,)),
        ],
        compiler_params=pltpu.CompilerParams(vmem_limit_bytes=SMALL_VMEM),
        cost_estimate=pl.CostEstimate(flops=2 * 4096 * 512 * 256, bytes_accessed=5 << 20, transcendentals=0),
        name="local_sums",
    )(got, ghosts, columns, *ops)


def body(weights, leaves, m2l_ops, send_index, pair_target, pair_source, pair_count):
    send = jnp.transpose(send_index, (0, 2, 1)).reshape(GHOST, SEG)
    parents, message, own, side, across = upward(leaves, pair_target, pair_source, pair_count, send, weights, m2l_ops)
    got = lax.all_to_all(message, ("c", "x"), 0, 0, tiled=True)
    across = lax.ppermute(across, "x", [(i, (i + 2) % SUBS) for i in range(SUBS)])
    steps = [(c * SUBS + i, c * SUBS + (i + 3 + 2 * c) % SUBS) for c in range(2) for i in range(SUBS)]
    side = lax.ppermute(side, ("c", "x"), steps)
    swapped = lax.ppermute(side[1], "c", [(0, 1), (1, 0)])
    ghosts = lax.all_to_all(pick(got), ("y", "z"), 0, 0, tiled=True)
    columns = plan(got, side, across)
    ops = (own, side, across, swapped)
    sums = local_sums(got, ghosts, columns, ops)
    parts = lax.all_to_all(sums, ("c", "x"), 0, 0, tiled=True)
    local = jnp.sum(parts.reshape(PEERS, ROWS, NODES).astype(F32), axis=0)
    return (parents, local)


def solution(mesh):
    four = Mesh(mesh.devices.reshape(8, 8, 2, SUBS), ("y", "z", "c", "x"))
    slab = ("y", "z", "c")
    every = slab + ("x",)
    in_specs = (
        P(every, None),
        P("x", None, None),
        P(slab, None, None),
        P(slab, "x", None),
        P(slab, "x", None),
        P(slab, "x"),
    )
    out_specs = (P(every, None), P(every, None))
    weights = upward_matrix()
    return jax.shard_map(
        lambda *args: body(jnp.asarray(weights), *args), mesh=four, in_specs=in_specs, out_specs=out_specs, check_vma=False
    )
```

```python
import functools
import math

import jax
import jax.numpy as jnp
import numpy as np
from jax import lax
from jax.experimental import pallas as pl
from jax.experimental.pallas import tpu as pltpu
from jax.sharding import Mesh, PartitionSpec as P

ORDER = 8
NODES = 512
SEG = 128
GHOST = 8
TABLE = 1152
BASE = 32
CHIPS = 64
SUBS = 4
PEERS = 8
ROWS = 32
MSG = 48
OURS, THEIRS = 640, 384
EIGHTH = 64
LANES = 128
WIDTH = 384
PLAN_FLOPS = 1 << 34
VMEM = 60 << 20
SMALL_VMEM = 16 << 20
BF = jnp.bfloat16
F32 = jnp.float32


def one_side(side):
    counter = np.arange(ORDER, dtype=np.float32)
    angles = (np.float32(2.0) * counter + np.float32(1.0)) * np.float32(math.pi) / np.float32(2.0 * ORDER)
    nodes = np.cos(angles)
    degree = np.arange(1, ORDER, dtype=np.float32)
    parent_poly = np.cos(degree[:, None] * angles[None, :])
    child_pts = (nodes + np.float32(2.0 * side - 1.0)) / np.float32(2.0)
    child_poly = np.cos(degree[:, None] * np.arccos(child_pts)[None, :])
    summed = np.sum(parent_poly[:, :, None] * child_poly[:, None, :], axis=0)
    return (np.float32(1.0 / ORDER) + np.float32(2.0 / ORDER) * summed).astype(np.float32)


def upward_factors():
    sides = [one_side(0), one_side(1)]
    inner = [np.kron(np.eye(2), np.kron(sides[i >> 1], sides[i & 1]).T) for i in range(4)]
    outer = [np.kron(side.T, np.eye(EIGHTH)) for side in sides]
    inner = np.concatenate(inner).astype(np.float32)
    high = inner.astype(BF)
    low = (inner - high.astype(np.float32)).astype(BF)
    return np.concatenate([high, low], axis=1), np.concatenate(outer).astype(BF)


def dot(a, b):
    return lax.dot_general(a, b, (((1,), (0,)), ((), ())), preferred_element_type=F32)


def dot_t(a, b):
    return lax.dot_general(a, b, (((1,), (1,)), ((), ())), preferred_element_type=F32)


def iota(shape, axis):
    return lax.broadcasted_iota(jnp.int32, shape, axis)


def onehot(flags):
    return jnp.where(flags, 1.0, 0.0).astype(BF)


def upward_kernel(
    count_hbm, leaves_hbm, target_hbm, source_hbm, send_hbm, inner_hbm, outer_hbm, ops_hbm,
    parents_ref, msg_ref, own_hbm, side_hbm, across_hbm,
    count_ref, leaves_ref, target_ref, source_ref, send_ref, inner_ref, outer_ref, own_ref, side_ref, across_ref, sems, out_sems,
):
    sub, core = lax.axis_index("x"), lax.axis_index("c")
    own, beside, across = [pl.multiple_of((x & 3) * LANES, LANES) for x in (sub, sub + 3 + 2 * core, sub + 2)]
    small = ((count_hbm, count_ref), (target_hbm, target_ref), (source_hbm, source_ref), (send_hbm, send_ref))
    copies = [pltpu.make_async_copy(source, to, sems.at[i]) for i, (source, to) in enumerate(small)]
    copies += [pltpu.make_async_copy(leaves_hbm, leaves_ref, sems.at[4])]
    copies += [pltpu.make_async_copy(inner_hbm, inner_ref, sems.at[5]), pltpu.make_async_copy(outer_hbm, outer_ref, sems.at[6])]
    for copy in copies:
        copy.start()
    into = [
        pltpu.make_async_copy(ops_hbm.at[:, :, pl.ds(beside, LANES)], side_ref, out_sems.at[0]),
        pltpu.make_async_copy(ops_hbm.at[pl.ds(2 * core, 2), :, pl.ds(across, LANES)], across_ref, out_sems.at[1]),
        pltpu.make_async_copy(ops_hbm.at[:, :, pl.ds(own, LANES)], own_ref, out_sems.at[2]),
    ]
    out = [
        pltpu.make_async_copy(side_ref, side_hbm, out_sems.at[3]),
        pltpu.make_async_copy(across_ref, across_hbm, out_sems.at[4]),
        pltpu.make_async_copy(own_ref, own_hbm, out_sems.at[5]),
    ]
    for copy in into:
        copy.start()
    to, at = iota((256, 256), 0), iota((256, 256), 1)
    sort = onehot(at == (to & 31) * 8 + (to >> 5))
    for copy in copies[:4]:
        copy.wait()
    slot = iota((1, SEG), 1)
    row = iota((8, SEG), 0)
    digits, matches = [], []
    for k in range(4):
        live = slot < count_ref[0:1, k : k + 1]
        target = jnp.where(live, target_ref[0, k : k + 1, :], -1)
        source = source_ref[0, k : k + 1, :]
        high = jnp.where(live, (source >> 5) + 1, 0).astype(F32)
        low = jnp.where(live, source & (BASE - 1), 0).astype(F32)
        digits.append(jnp.where(row == k, high, jnp.where(row == 4 + k, low, 0.0)).astype(BF))
        matches.append(onehot(iota((SEG, SEG), 0) == target))
    info = dot_t(jnp.concatenate(digits, axis=1), jnp.concatenate(matches, axis=1))
    tail = jnp.concatenate([send_ref[...].astype(F32), info], axis=0).astype(BF)
    for e in range(PEERS):
        msg_ref[e, ROWS:MSG, :] = tail
    for i in range(3):
        into[i].wait()
        out[i].start()
    copies[4].wait()
    sorted_leaves = dot(sort, leaves_ref[...]).astype(BF)
    copies[5].wait()
    lhs = []
    for x in range(2):
        for j in range(4):
            parts = [sorted_leaves[(4 * x + i) * ROWS : (4 * x + i + 1) * ROWS, j * LANES : (j + 1) * LANES] for i in range(4)]
            lhs.append(jnp.concatenate(parts, axis=1))
    both = dot(jnp.concatenate(lhs, axis=0), inner_ref[...])
    partial = both[:, 0:LANES] + both[:, LANES:]
    partial = jnp.concatenate([partial[i * ROWS : (i + 1) * ROWS, :] for i in range(8)], axis=1)
    high = partial.astype(BF)
    low = (partial - high.astype(F32)).astype(BF)
    copies[6].wait()
    total = dot(jnp.concatenate([high, low], axis=0), outer_ref[...])
    total = total[0:ROWS, :] + total[ROWS:, :]
    parents = total.astype(BF)
    parents_ref[...] = parents
    wide = parents.astype(F32)
    lane = iota((ROWS, LANES), 1)
    for j in range(SUBS):
        block = wide[:, j * LANES : (j + 1) * LANES]
        turned = pltpu.roll(block, EIGHTH, 1)
        msg_ref[j, 0:ROWS, :] = jnp.where(lane < EIGHTH, block, turned).astype(BF)
        msg_ref[SUBS + j, 0:ROWS, :] = jnp.where(lane < EIGHTH, turned, block).astype(BF)
    for copy in out:
        copy.wait()


def upward(leaves, target, source, count, send, factors, ops):
    vmem, anywhere = pl.BlockSpec(memory_space=pltpu.VMEM), pl.BlockSpec(memory_space=pl.ANY)
    return pl.pallas_call(
        upward_kernel,
        out_shape=(
            jax.ShapeDtypeStruct((ROWS, NODES), BF),
            jax.ShapeDtypeStruct((PEERS, MSG, LANES), BF),
            jax.ShapeDtypeStruct((4, NODES, LANES), BF),
            jax.ShapeDtypeStruct((4, NODES, LANES), BF),
            jax.ShapeDtypeStruct((2, NODES, LANES), BF),
        ),
        in_specs=[anywhere] * 8,
        out_specs=(vmem, vmem, anywhere, anywhere, anywhere),
        scratch_shapes=[
            pltpu.VMEM((1, 4), jnp.int32),
            pltpu.VMEM((256, NODES), BF),
            pltpu.VMEM((1, 4, SEG), jnp.int32),
            pltpu.VMEM((1, 4, SEG), jnp.int32),
            pltpu.VMEM((GHOST, SEG), jnp.int32),
            pltpu.VMEM((4 * LANES, 2 * LANES), BF),
            pltpu.VMEM((2 * NODES, NODES), BF),
            pltpu.VMEM((4, NODES, LANES), BF),
            pltpu.VMEM((4, NODES, LANES), BF),
            pltpu.VMEM((2, NODES, LANES), BF),
            pltpu.SemaphoreType.DMA((7,)),
            pltpu.SemaphoreType.DMA((6,)),
        ],
        compiler_params=pltpu.CompilerParams(vmem_limit_bytes=VMEM),
        cost_estimate=pl.CostEstimate(flops=2 * 256 * 512 * 512, bytes_accessed=5 << 20, transcendentals=0),
        name="upward",
    )(count, leaves, target, source, send, *factors, ops)


def pick_kernel(got_ref, out_ref):
    parents = jnp.concatenate([got_ref[j, 0:ROWS, :] for j in range(PEERS)], axis=0)
    lane = iota((2 * SEG, LANES), 1)
    zero = jnp.zeros_like(parents)
    rhs = jnp.concatenate([jnp.where(lane < EIGHTH, parents, zero), jnp.where(lane < EIGHTH, zero, parents)], axis=0)
    send = jnp.concatenate([got_ref[0, ROWS : ROWS + 8, :].astype(F32), got_ref[4, ROWS : ROWS + 8, :].astype(F32) + SEG], axis=0)
    send = send.astype(jnp.int32)
    at = iota((16, 2 * SEG), 1)
    step = 16
    for first in range(0, CHIPS, step):
        blocks = []
        for d in range(first, first + step):
            halves = [onehot(send[:, 2 * d + h : 2 * d + h + 1] == at) for h in range(2)]
            blocks.append(jnp.concatenate(halves, axis=1))
        lhs = jnp.concatenate(blocks, axis=0)
        out_ref[first * 16 : (first + step) * 16, :] = dot(lhs, rhs).astype(BF)


def pick(got):
    vmem = pl.BlockSpec(memory_space=pltpu.VMEM)
    return pl.pallas_call(
        pick_kernel,
        out_shape=jax.ShapeDtypeStruct((CHIPS * 16, LANES), BF),
        in_specs=[vmem],
        out_specs=vmem,
        compiler_params=pltpu.CompilerParams(vmem_limit_bytes=SMALL_VMEM),
        cost_estimate=pl.CostEstimate(flops=PLAN_FLOPS, bytes_accessed=1 << 19, transcendentals=0),
        name="pick",
    )(got)


def plan_kernel(got_ref, own_ref, side_ref, across_ref, out_ref, ours_ref, theirs_ref):
    sub, core = lax.axis_index("x"), lax.axis_index("c")
    beside = (sub + 1 + 2 * core, sub + 3 + 2 * core)
    for q in range(2):
        groups = []
        for x in (sub, beside[0], beside[1], sub + 2):
            info = got_ref[q * 4 + (x & 3), ROWS + 8 : MSG, :].astype(F32)
            groups.append(((info[0:4, :] - 1.0) * BASE + info[4:8, :]).astype(jnp.int32))
        first, last = groups[3][0:2, :], groups[3][2:4, :]
        here, there = jnp.where(core == 0, first, last), jnp.where(core == 0, last, first)
        at = q * 16
        for source in (groups[0], groups[1], here, groups[2], there):
            rows = source.shape[0]
            ghost = source - SEG
            out_ref[at : at + rows, :] = jnp.where(source < SEG, jnp.where(source < 0, -1, source + 256), ghost & 255)
            out_ref[32 + at : 32 + at + rows, :] = jnp.where(source < SEG, 0, ghost >> 8)
            at += rows
    to, at = iota((EIGHTH, LANES), 0), iota((EIGHTH, LANES), 1)
    mine, other = onehot(at == core * EIGHTH + to), onehot(at == (1 - core) * EIGHTH + to)
    for k in range(6):
        tile = side_ref[k] if k < 4 else across_ref[k - 4]
        theirs_ref[k * EIGHTH : (k + 1) * EIGHTH, :] = dot_t(other, tile).astype(BF)
        ours_ref[(4 + k) * EIGHTH : (5 + k) * EIGHTH, :] = dot_t(mine, tile).astype(BF)
    for k in range(4):
        ours_ref[k * EIGHTH : (k + 1) * EIGHTH, :] = dot_t(mine, own_ref[k]).astype(BF)


def plan(got, own, side, across):
    vmem, anywhere = pl.BlockSpec(memory_space=pltpu.VMEM), pl.BlockSpec(memory_space=pl.ANY)
    return pl.pallas_call(
        plan_kernel,
        out_shape=(
            jax.ShapeDtypeStruct((64, SEG), jnp.int32),
            jax.ShapeDtypeStruct((OURS, NODES), BF),
            jax.ShapeDtypeStruct((THEIRS, NODES), BF),
        ),
        in_specs=[vmem] * 4,
        out_specs=(vmem, vmem, vmem),
        compiler_params=pltpu.CompilerParams(vmem_limit_bytes=SMALL_VMEM),
        cost_estimate=pl.CostEstimate(flops=PLAN_FLOPS, bytes_accessed=5 << 20, transcendentals=0),
        name="plan",
    )(got, own, side, across)


def local_kernel(got_ref, ghosts_ref, plan_ref, ours_hbm, theirs_hbm, out_ref, m_ref, rows_ref, rhs_ref, x_ref, sems):
    copies = [
        pltpu.make_async_copy(ours_hbm, m_ref.at[0:OURS], sems.at[0]),
        pltpu.make_async_copy(theirs_hbm, m_ref.at[OURS:1024], sems.at[1]),
    ]
    for copy in copies:
        copy.start()
    row = iota((WIDTH, SEG), 0)
    for q in range(2):
        for k in range(16):
            at = q * 16 + k
            rows_ref[q, :, k * SEG : (k + 1) * SEG] = onehot(plan_ref[at : at + 1, :] == row)
    for q in range(2):
        own = jnp.concatenate([got_ref[q * 4 + j, 0:ROWS, 0:EIGHTH] for j in range(4)], axis=0).astype(F32).T
        rhs_ref[q, 0:EIGHTH, 256:WIDTH] = own.astype(BF)
        rhs_ref[q, EIGHTH:256, 256:WIDTH] = jnp.zeros((256 - EIGHTH, SEG), BF)
    for b in range(4):
        block = ghosts_ref[b * 256 : (b + 1) * 256, :].astype(F32).T.astype(BF)
        rhs_ref[0, b * EIGHTH : (b + 1) * EIGHTH, 0:256] = block[0:EIGHTH, :]
        rhs_ref[1, b * EIGHTH : (b + 1) * EIGHTH, 0:256] = block[EIGHTH:LANES, :]
    for q in range(2):
        for k in range(0, 16, 2):
            both = dot(rhs_ref[q], rows_ref[q, :, k * SEG : (k + 2) * SEG])
            for i in range(k, k + 2):
                at = 32 + q * 16 + i
                block = plan_ref[at : at + 1, :]
                part = both[:, (i - k) * SEG : (i - k + 1) * SEG]
                kept = jnp.where(block == 0, part[0:EIGHTH, :], 0.0)
                for b in range(1, 4):
                    kept = jnp.where(block == b, part[b * EIGHTH : (b + 1) * EIGHTH, :], kept)
                x_ref[i * EIGHTH : (i + 1) * EIGHTH, q * SEG : (q + 1) * SEG] = kept.astype(BF)
    for copy in copies:
        copy.wait()
    total = lax.dot_general(x_ref[...], m_ref[...], (((0,), (0,)), ((), ())), preferred_element_type=F32)
    out_ref[...] = total.astype(BF)


def local_sums(got, ghosts, columns, ours, theirs):
    vmem, anywhere = pl.BlockSpec(memory_space=pltpu.VMEM), pl.BlockSpec(memory_space=pl.ANY)
    return pl.pallas_call(
        local_kernel,
        out_shape=jax.ShapeDtypeStruct((2 * SEG, NODES), BF),
        in_specs=[vmem] * 3 + [anywhere] * 2,
        out_specs=vmem,
        scratch_shapes=[
            pltpu.VMEM((1024, NODES), BF),
            pltpu.VMEM((2, WIDTH, 16 * SEG), BF),
            pltpu.VMEM((2, 256, WIDTH), BF),
            pltpu.VMEM((1024, 2 * SEG), BF),
            pltpu.SemaphoreType.DMA((2,)),
        ],
        compiler_params=pltpu.CompilerParams(vmem_limit_bytes=SMALL_VMEM),
        cost_estimate=pl.CostEstimate(flops=2 * 4096 * 512 * 256, bytes_accessed=5 << 20, transcendentals=0),
        name="local_sums",
    )(got, ghosts, columns, ours, theirs)


def body(factors, leaves, m2l_ops, send_index, pair_target, pair_source, pair_count):
    send = jnp.transpose(send_index, (0, 2, 1)).reshape(GHOST, SEG)
    parents, message, own, side, across = upward(leaves, pair_target, pair_source, pair_count, send, factors, m2l_ops)
    got = lax.all_to_all(message, ("c", "x"), 0, 0, tiled=True)
    steps = [(c * SUBS + i, c * SUBS + (i + 3 + 2 * c) % SUBS) for c in range(2) for i in range(SUBS)]
    side = lax.ppermute(side, ("c", "x"), steps)
    across = lax.ppermute(across, "x", [(i, (i + 2) % SUBS) for i in range(SUBS)])
    ghosts = lax.all_to_all(pick(got), ("y", "z"), 0, 0, tiled=True)
    columns, ours, theirs = plan(got, own, side, across)
    theirs = lax.ppermute(theirs, "c", [(0, 1), (1, 0)])
    sums = local_sums(got, ghosts, columns, ours, theirs)
    parts = lax.all_to_all(sums, ("c", "x"), 0, 0, tiled=True)
    local = jnp.sum(parts.reshape(PEERS, ROWS, NODES).astype(F32), axis=0)
    return (parents, local)


def solution(mesh):
    four = Mesh(mesh.devices.reshape(8, 8, 2, SUBS), ("y", "z", "c", "x"))
    slab = ("y", "z", "c")
    every = slab + ("x",)
    in_specs = (
        P(every, None),
        P("x", None, None),
        P(slab, None, None),
        P(slab, "x", None),
        P(slab, "x", None),
        P(slab, "x"),
    )
    out_specs = (P(every, None), P(every, None))
    factors = upward_factors()
    return jax.shard_map(
        lambda *args: body([jnp.asarray(factor) for factor in factors], *args), mesh=four, in_specs=in_specs, out_specs=out_specs, check_vma=False
    )
```

```python
import functools
import math

import jax
import jax.numpy as jnp
import numpy as np
from jax import lax
from jax.experimental import pallas as pl
from jax.experimental.pallas import tpu as pltpu
from jax.sharding import Mesh, PartitionSpec as P

ORDER = 8
NODES = 512
SEG = 128
GHOST = 8
TABLE = 1152
BASE = 32
CHIPS = 64
SUBS = 4
PEERS = 8
ROWS = 32
MSG = 48
OURS, THEIRS = 640, 384
EIGHTH = 64
LANES = 128
WIDTH = 384
PLAN_FLOPS = 1 << 34
VMEM = 60 << 20
SMALL_VMEM = 16 << 20
BF = jnp.bfloat16
F32 = jnp.float32


def one_side(side):
    counter = np.arange(ORDER, dtype=np.float32)
    angles = (np.float32(2.0) * counter + np.float32(1.0)) * np.float32(math.pi) / np.float32(2.0 * ORDER)
    nodes = np.cos(angles)
    degree = np.arange(1, ORDER, dtype=np.float32)
    parent_poly = np.cos(degree[:, None] * angles[None, :])
    child_pts = (nodes + np.float32(2.0 * side - 1.0)) / np.float32(2.0)
    child_poly = np.cos(degree[:, None] * np.arccos(child_pts)[None, :])
    summed = np.sum(parent_poly[:, :, None] * child_poly[:, None, :], axis=0)
    return (np.float32(1.0 / ORDER) + np.float32(2.0 / ORDER) * summed).astype(np.float32)


def upward_factors():
    sides = [one_side(0), one_side(1)]
    inner = [np.kron(np.eye(2), np.kron(sides[i >> 1], sides[i & 1]).T) for i in range(4)]
    outer = [np.kron(side.T, np.eye(EIGHTH)) for side in sides]
    inner = np.concatenate(inner).astype(np.float32)
    high = inner.astype(BF)
    low = (inner - high.astype(np.float32)).astype(BF)
    return np.concatenate([high, low], axis=1), np.concatenate(outer).astype(BF)


def dot(a, b):
    return lax.dot_general(a, b, (((1,), (0,)), ((), ())), preferred_element_type=F32)


def dot_t(a, b):
    return lax.dot_general(a, b, (((1,), (1,)), ((), ())), preferred_element_type=F32)


def iota(shape, axis):
    return lax.broadcasted_iota(jnp.int32, shape, axis)


def onehot(flags):
    return jnp.where(flags, 1.0, 0.0).astype(BF)


def upward_kernel(
    count_hbm, leaves_hbm, target_hbm, source_hbm, send_hbm, inner_hbm, outer_hbm, ops_hbm,
    parents_ref, msg_ref, own_ref, side_ref, across_ref,
    count_ref, leaves_ref, target_ref, source_ref, send_ref, inner_ref, outer_ref, sems, out_sems,
):
    sub, core = lax.axis_index("x"), lax.axis_index("c")
    own, beside, across = [pl.multiple_of((x & 3) * LANES, LANES) for x in (sub, sub + 3 + 2 * core, sub + 2)]
    small = ((count_hbm, count_ref), (target_hbm, target_ref), (source_hbm, source_ref), (send_hbm, send_ref))
    copies = [pltpu.make_async_copy(source, to, sems.at[i]) for i, (source, to) in enumerate(small)]
    copies += [pltpu.make_async_copy(leaves_hbm, leaves_ref, sems.at[4])]
    copies += [pltpu.make_async_copy(inner_hbm, inner_ref, sems.at[5]), pltpu.make_async_copy(outer_hbm, outer_ref, sems.at[6])]
    for copy in copies:
        copy.start()
    into = [
        pltpu.make_async_copy(ops_hbm.at[:, :, pl.ds(beside, LANES)], side_ref, out_sems.at[0]),
        pltpu.make_async_copy(ops_hbm.at[pl.ds(2 * core, 2), :, pl.ds(across, LANES)], across_ref, out_sems.at[1]),
        pltpu.make_async_copy(ops_hbm.at[:, :, pl.ds(own, LANES)], own_ref, out_sems.at[2]),
    ]
    for copy in into:
        copy.start()
    to, at = iota((256, 256), 0), iota((256, 256), 1)
    sort = onehot(at == (to & 31) * 8 + (to >> 5))
    for copy in copies[:4]:
        copy.wait()
    slot = iota((1, SEG), 1)
    row = iota((8, SEG), 0)
    digits, matches = [], []
    for k in range(4):
        live = slot < count_ref[0:1, k : k + 1]
        target = jnp.where(live, target_ref[0, k : k + 1, :], -1)
        source = source_ref[0, k : k + 1, :]
        high = jnp.where(live, (source >> 5) + 1, 0).astype(F32)
        low = jnp.where(live, source & (BASE - 1), 0).astype(F32)
        digits.append(jnp.where(row == k, high, jnp.where(row == 4 + k, low, 0.0)).astype(BF))
        matches.append(onehot(iota((SEG, SEG), 0) == target))
    info = dot_t(jnp.concatenate(digits, axis=1), jnp.concatenate(matches, axis=1))
    tail = jnp.concatenate([send_ref[...].astype(F32), info], axis=0).astype(BF)
    for e in range(PEERS):
        msg_ref[e, ROWS:MSG, :] = tail
    copies[4].wait()
    sorted_leaves = dot(sort, leaves_ref[...]).astype(BF)
    copies[5].wait()
    lhs = []
    for x in range(2):
        for j in range(4):
            parts = [sorted_leaves[(4 * x + i) * ROWS : (4 * x + i + 1) * ROWS, j * LANES : (j + 1) * LANES] for i in range(4)]
            lhs.append(jnp.concatenate(parts, axis=1))
    both = dot(jnp.concatenate(lhs, axis=0), inner_ref[...])
    partial = both[:, 0:LANES] + both[:, LANES:]
    partial = jnp.concatenate([partial[i * ROWS : (i + 1) * ROWS, :] for i in range(8)], axis=1)
    high = partial.astype(BF)
    low = (partial - high.astype(F32)).astype(BF)
    copies[6].wait()
    total = dot(jnp.concatenate([high, low], axis=0), outer_ref[...])
    total = total[0:ROWS, :] + total[ROWS:, :]
    parents = total.astype(BF)
    parents_ref[...] = parents
    wide = parents.astype(F32)
    lane = iota((ROWS, LANES), 1)
    for j in range(SUBS):
        block = wide[:, j * LANES : (j + 1) * LANES]
        turned = pltpu.roll(block, EIGHTH, 1)
        msg_ref[j, 0:ROWS, :] = jnp.where(lane < EIGHTH, block, turned).astype(BF)
        msg_ref[SUBS + j, 0:ROWS, :] = jnp.where(lane < EIGHTH, turned, block).astype(BF)
    for copy in into:
        copy.wait()


def upward(leaves, target, source, count, send, factors, ops):
    vmem, anywhere = pl.BlockSpec(memory_space=pltpu.VMEM), pl.BlockSpec(memory_space=pl.ANY)
    return pl.pallas_call(
        upward_kernel,
        out_shape=(
            jax.ShapeDtypeStruct((ROWS, NODES), BF),
            pltpu.VMEM((PEERS, MSG, LANES), BF),
            pltpu.VMEM((4, NODES, LANES), BF),
            pltpu.VMEM((4, NODES, LANES), BF),
            pltpu.VMEM((2, NODES, LANES), BF),
        ),
        in_specs=[anywhere] * 8,
        out_specs=(vmem,) * 5,
        scratch_shapes=[
            pltpu.VMEM((1, 4), jnp.int32),
            pltpu.VMEM((256, NODES), BF),
            pltpu.VMEM((1, 4, SEG), jnp.int32),
            pltpu.VMEM((1, 4, SEG), jnp.int32),
            pltpu.VMEM((GHOST, SEG), jnp.int32),
            pltpu.VMEM((4 * LANES, 2 * LANES), BF),
            pltpu.VMEM((2 * NODES, NODES), BF),
            pltpu.SemaphoreType.DMA((7,)),
            pltpu.SemaphoreType.DMA((3,)),
        ],
        compiler_params=pltpu.CompilerParams(vmem_limit_bytes=VMEM),
        cost_estimate=pl.CostEstimate(flops=2 * 256 * 512 * 512, bytes_accessed=5 << 20, transcendentals=0),
        name="upward",
    )(count, leaves, target, source, send, *factors, ops)


def pick_kernel(got_ref, out_ref):
    parents = jnp.concatenate([got_ref[j, 0:ROWS, :] for j in range(PEERS)], axis=0)
    lane = iota((2 * SEG, LANES), 1)
    zero = jnp.zeros_like(parents)
    rhs = jnp.concatenate([jnp.where(lane < EIGHTH, parents, zero), jnp.where(lane < EIGHTH, zero, parents)], axis=0)
    send = jnp.concatenate([got_ref[0, ROWS : ROWS + 8, :].astype(F32), got_ref[4, ROWS : ROWS + 8, :].astype(F32) + SEG], axis=0)
    send = send.astype(jnp.int32)
    at = iota((16, 2 * SEG), 1)
    step = 16
    for first in range(0, CHIPS, step):
        blocks = []
        for d in range(first, first + step):
            halves = [onehot(send[:, 2 * d + h : 2 * d + h + 1] == at) for h in range(2)]
            blocks.append(jnp.concatenate(halves, axis=1))
        lhs = jnp.concatenate(blocks, axis=0)
        out_ref[first * 16 : (first + step) * 16, :] = dot(lhs, rhs).astype(BF)


def pick(got):
    vmem = pl.BlockSpec(memory_space=pltpu.VMEM)
    return pl.pallas_call(
        pick_kernel,
        out_shape=pltpu.VMEM((CHIPS * 16, LANES), BF),
        in_specs=[vmem],
        out_specs=vmem,
        compiler_params=pltpu.CompilerParams(vmem_limit_bytes=SMALL_VMEM),
        cost_estimate=pl.CostEstimate(flops=PLAN_FLOPS, bytes_accessed=1 << 19, transcendentals=0),
        name="pick",
    )(got)


def plan_kernel(got_ref, own_ref, side_ref, across_ref, out_ref, ours_ref, theirs_ref):
    sub, core = lax.axis_index("x"), lax.axis_index("c")
    beside = (sub + 1 + 2 * core, sub + 3 + 2 * core)
    for q in range(2):
        groups = []
        for x in (sub, beside[0], beside[1], sub + 2):
            info = got_ref[q * 4 + (x & 3), ROWS + 8 : MSG, :].astype(F32)
            groups.append(((info[0:4, :] - 1.0) * BASE + info[4:8, :]).astype(jnp.int32))
        first, last = groups[3][0:2, :], groups[3][2:4, :]
        here, there = jnp.where(core == 0, first, last), jnp.where(core == 0, last, first)
        at = q * 16
        for source in (groups[0], groups[1], here, groups[2], there):
            rows = source.shape[0]
            ghost = source - SEG
            out_ref[at : at + rows, :] = jnp.where(source < SEG, jnp.where(source < 0, -1, source + 256), ghost & 255)
            out_ref[32 + at : 32 + at + rows, :] = jnp.where(source < SEG, 0, ghost >> 8)
            at += rows
    to, at = iota((EIGHTH, LANES), 0), iota((EIGHTH, LANES), 1)
    mine, other = onehot(at == core * EIGHTH + to), onehot(at == (1 - core) * EIGHTH + to)
    for k in range(6):
        tile = side_ref[k] if k < 4 else across_ref[k - 4]
        theirs_ref[k * EIGHTH : (k + 1) * EIGHTH, :] = dot_t(other, tile).astype(BF)
        ours_ref[(4 + k) * EIGHTH : (5 + k) * EIGHTH, :] = dot_t(mine, tile).astype(BF)
    for k in range(4):
        ours_ref[k * EIGHTH : (k + 1) * EIGHTH, :] = dot_t(mine, own_ref[k]).astype(BF)


def plan(got, own, side, across):
    vmem, anywhere = pl.BlockSpec(memory_space=pltpu.VMEM), pl.BlockSpec(memory_space=pl.ANY)
    return pl.pallas_call(
        plan_kernel,
        out_shape=(
            jax.ShapeDtypeStruct((64, SEG), jnp.int32),
            jax.ShapeDtypeStruct((OURS, NODES), BF),
            jax.ShapeDtypeStruct((THEIRS, NODES), BF),
        ),
        in_specs=[vmem] * 4,
        out_specs=(vmem, vmem, vmem),
        compiler_params=pltpu.CompilerParams(vmem_limit_bytes=SMALL_VMEM),
        cost_estimate=pl.CostEstimate(flops=PLAN_FLOPS, bytes_accessed=5 << 20, transcendentals=0),
        name="plan",
    )(got, own, side, across)


def local_kernel(got_ref, ghosts_ref, plan_ref, ours_hbm, theirs_hbm, out_ref, m_ref, rows_ref, rhs_ref, x_ref, sems):
    copies = [
        pltpu.make_async_copy(ours_hbm, m_ref.at[0:OURS], sems.at[0]),
        pltpu.make_async_copy(theirs_hbm, m_ref.at[OURS:1024], sems.at[1]),
    ]
    for copy in copies:
        copy.start()
    row = iota((WIDTH, SEG), 0)
    for q in range(2):
        for k in range(16):
            at = q * 16 + k
            rows_ref[q, :, k * SEG : (k + 1) * SEG] = onehot(plan_ref[at : at + 1, :] == row)
    for q in range(2):
        own = jnp.concatenate([got_ref[q * 4 + j, 0:ROWS, 0:EIGHTH] for j in range(4)], axis=0).astype(F32).T
        rhs_ref[q, 0:EIGHTH, 256:WIDTH] = own.astype(BF)
        rhs_ref[q, EIGHTH:256, 256:WIDTH] = jnp.zeros((256 - EIGHTH, SEG), BF)
    for b in range(4):
        block = ghosts_ref[b * 256 : (b + 1) * 256, :].astype(F32).T.astype(BF)
        rhs_ref[0, b * EIGHTH : (b + 1) * EIGHTH, 0:256] = block[0:EIGHTH, :]
        rhs_ref[1, b * EIGHTH : (b + 1) * EIGHTH, 0:256] = block[EIGHTH:LANES, :]
    for q in range(2):
        for k in range(0, 16, 2):
            both = dot(rhs_ref[q], rows_ref[q, :, k * SEG : (k + 2) * SEG])
            for i in range(k, k + 2):
                at = 32 + q * 16 + i
                block = plan_ref[at : at + 1, :]
                part = both[:, (i - k) * SEG : (i - k + 1) * SEG]
                kept = jnp.where(block == 0, part[0:EIGHTH, :], 0.0)
                for b in range(1, 4):
                    kept = jnp.where(block == b, part[b * EIGHTH : (b + 1) * EIGHTH, :], kept)
                x_ref[i * EIGHTH : (i + 1) * EIGHTH, q * SEG : (q + 1) * SEG] = kept.astype(BF)
    for copy in copies:
        copy.wait()
    total = lax.dot_general(x_ref[...], m_ref[...], (((0,), (0,)), ((), ())), preferred_element_type=F32)
    out_ref[...] = total.astype(BF)


def local_sums(got, ghosts, columns, ours, theirs):
    vmem, anywhere = pl.BlockSpec(memory_space=pltpu.VMEM), pl.BlockSpec(memory_space=pl.ANY)
    return pl.pallas_call(
        local_kernel,
        out_shape=jax.ShapeDtypeStruct((2 * SEG, NODES), BF),
        in_specs=[vmem] * 3 + [anywhere] * 2,
        out_specs=vmem,
        scratch_shapes=[
            pltpu.VMEM((1024, NODES), BF),
            pltpu.VMEM((2, WIDTH, 16 * SEG), BF),
            pltpu.VMEM((2, 256, WIDTH), BF),
            pltpu.VMEM((1024, 2 * SEG), BF),
            pltpu.SemaphoreType.DMA((2,)),
        ],
        compiler_params=pltpu.CompilerParams(vmem_limit_bytes=SMALL_VMEM),
        cost_estimate=pl.CostEstimate(flops=2 * 4096 * 512 * 256, bytes_accessed=5 << 20, transcendentals=0),
        name="local_sums",
    )(got, ghosts, columns, ours, theirs)


def body(factors, leaves, m2l_ops, send_index, pair_target, pair_source, pair_count):
    send = jnp.transpose(send_index, (0, 2, 1)).reshape(GHOST, SEG)
    parents, message, own, side, across = upward(leaves, pair_target, pair_source, pair_count, send, factors, m2l_ops)
    got = lax.all_to_all(message, ("c", "x"), 0, 0, tiled=True)
    steps = [(c * SUBS + i, c * SUBS + (i + 3 + 2 * c) % SUBS) for c in range(2) for i in range(SUBS)]
    side = lax.ppermute(side, ("c", "x"), steps)
    across = lax.ppermute(across, "x", [(i, (i + 2) % SUBS) for i in range(SUBS)])
    ghosts = lax.all_to_all(pick(got), ("y", "z"), 0, 0, tiled=True)
    columns, ours, theirs = plan(got, own, side, across)
    theirs = lax.ppermute(theirs, "c", [(0, 1), (1, 0)])
    sums = local_sums(got, ghosts, columns, ours, theirs)
    parts = lax.all_to_all(sums, ("c", "x"), 0, 0, tiled=True)
    local = jnp.sum(parts.reshape(PEERS, ROWS, NODES).astype(F32), axis=0)
    return (parents, local)


def solution(mesh):
    four = Mesh(mesh.devices.reshape(8, 8, 2, SUBS), ("y", "z", "c", "x"))
    slab = ("y", "z", "c")
    every = slab + ("x",)
    in_specs = (
        P(every, None),
        P("x", None, None),
        P(slab, None, None),
        P(slab, "x", None),
        P(slab, "x", None),
        P(slab, "x"),
    )
    out_specs = (P(every, None), P(every, None))
    factors = upward_factors()
    return jax.shard_map(
        lambda *args: body([jnp.asarray(factor) for factor in factors], *args), mesh=four, in_specs=in_specs, out_specs=out_specs, check_vma=False
    )
```

```python
import functools
import math

import jax
import jax.numpy as jnp
import numpy as np
from jax import lax
from jax.experimental import pallas as pl
from jax.experimental.pallas import tpu as pltpu
from jax.sharding import Mesh, PartitionSpec as P

ORDER = 8
NODES = 512
SEG = 128
GHOST = 8
TABLE = 1152
BASE = 32
CHIPS = 64
SUBS = 4
PEERS = 8
ROWS = 32
MSG = 48
EIGHTH = 64
LANES = 128
WIDTH = 384
PLAN_FLOPS = 1 << 34
VMEM = 60 << 20
SMALL_VMEM = 16 << 20
BF = jnp.bfloat16
F32 = jnp.float32


def one_side(side):
    counter = np.arange(ORDER, dtype=np.float32)
    angles = (np.float32(2.0) * counter + np.float32(1.0)) * np.float32(math.pi) / np.float32(2.0 * ORDER)
    nodes = np.cos(angles)
    degree = np.arange(1, ORDER, dtype=np.float32)
    parent_poly = np.cos(degree[:, None] * angles[None, :])
    child_pts = (nodes + np.float32(2.0 * side - 1.0)) / np.float32(2.0)
    child_poly = np.cos(degree[:, None] * np.arccos(child_pts)[None, :])
    summed = np.sum(parent_poly[:, :, None] * child_poly[:, None, :], axis=0)
    return (np.float32(1.0 / ORDER) + np.float32(2.0 / ORDER) * summed).astype(np.float32)


def upward_factors():
    sides = [one_side(0), one_side(1)]
    inner = [np.kron(np.eye(2), np.kron(sides[i >> 1], sides[i & 1]).T) for i in range(4)]
    outer = [np.kron(side.T, np.eye(EIGHTH)) for side in sides]
    inner = np.concatenate(inner).astype(np.float32)
    high = inner.astype(BF)
    low = (inner - high.astype(np.float32)).astype(BF)
    return np.concatenate([high, low], axis=1), np.concatenate(outer).astype(BF)


def dot(a, b):
    return lax.dot_general(a, b, (((1,), (0,)), ((), ())), preferred_element_type=F32)


def dot_t(a, b):
    return lax.dot_general(a, b, (((1,), (1,)), ((), ())), preferred_element_type=F32)


def iota(shape, axis):
    return lax.broadcasted_iota(jnp.int32, shape, axis)


def onehot(flags):
    return jnp.where(flags, 1.0, 0.0).astype(BF)


def upward_kernel(
    count_hbm, leaves_hbm, target_hbm, source_hbm, send_hbm, inner_hbm, outer_hbm, ops_hbm,
    parents_ref, msg_ref, own_ref, side_ref, across_ref,
    count_ref, leaves_ref, target_ref, source_ref, send_ref, inner_ref, outer_ref, sems, out_sems,
):
    sub, core = lax.axis_index("x"), lax.axis_index("c")
    own, beside, across = [pl.multiple_of((x & 3) * LANES, LANES) for x in (sub, sub + 3 + 2 * core, sub + 2)]
    small = ((count_hbm, count_ref), (target_hbm, target_ref), (source_hbm, source_ref), (send_hbm, send_ref))
    copies = [pltpu.make_async_copy(source, to, sems.at[i]) for i, (source, to) in enumerate(small)]
    copies += [pltpu.make_async_copy(leaves_hbm, leaves_ref, sems.at[4])]
    copies += [pltpu.make_async_copy(inner_hbm, inner_ref, sems.at[5]), pltpu.make_async_copy(outer_hbm, outer_ref, sems.at[6])]
    for copy in copies:
        copy.start()
    into = [
        pltpu.make_async_copy(ops_hbm.at[:, :, pl.ds(beside, LANES)], side_ref, out_sems.at[0]),
        pltpu.make_async_copy(ops_hbm.at[pl.ds(2 * core, 2), :, pl.ds(across, LANES)], across_ref, out_sems.at[1]),
        pltpu.make_async_copy(ops_hbm.at[:, :, pl.ds(own, LANES)], own_ref, out_sems.at[2]),
    ]
    for copy in into:
        copy.start()
    to, at = iota((256, 256), 0), iota((256, 256), 1)
    sort = onehot(at == (to & 31) * 8 + (to >> 5))
    for copy in copies[:4]:
        copy.wait()
    slot = iota((1, SEG), 1)
    row = iota((8, SEG), 0)
    digits, matches = [], []
    for k in range(4):
        live = slot < count_ref[0:1, k : k + 1]
        target = jnp.where(live, target_ref[0, k : k + 1, :], -1)
        source = source_ref[0, k : k + 1, :]
        high = jnp.where(live, (source >> 5) + 1, 0).astype(F32)
        low = jnp.where(live, source & (BASE - 1), 0).astype(F32)
        digits.append(jnp.where(row == k, high, jnp.where(row == 4 + k, low, 0.0)).astype(BF))
        matches.append(onehot(iota((SEG, SEG), 0) == target))
    info = dot_t(jnp.concatenate(digits, axis=1), jnp.concatenate(matches, axis=1))
    tail = jnp.concatenate([send_ref[...].astype(F32), info], axis=0).astype(BF)
    for e in range(PEERS):
        msg_ref[e, ROWS:MSG, :] = tail
    copies[4].wait()
    sorted_leaves = dot(sort, leaves_ref[...]).astype(BF)
    copies[5].wait()
    lhs = []
    for x in range(2):
        for j in range(4):
            parts = [sorted_leaves[(4 * x + i) * ROWS : (4 * x + i + 1) * ROWS, j * LANES : (j + 1) * LANES] for i in range(4)]
            lhs.append(jnp.concatenate(parts, axis=1))
    both = dot(jnp.concatenate(lhs, axis=0), inner_ref[...])
    partial = both[:, 0:LANES] + both[:, LANES:]
    partial = jnp.concatenate([partial[i * ROWS : (i + 1) * ROWS, :] for i in range(8)], axis=1)
    high = partial.astype(BF)
    low = (partial - high.astype(F32)).astype(BF)
    copies[6].wait()
    total = dot(jnp.concatenate([high, low], axis=0), outer_ref[...])
    total = total[0:ROWS, :] + total[ROWS:, :]
    parents = total.astype(BF)
    parents_ref[...] = parents
    for j in range(PEERS):
        msg_ref[j, 0:ROWS, :] = parents[:, (j & 3) * LANES : ((j & 3) + 1) * LANES]
    for copy in into:
        copy.wait()


def upward(leaves, target, source, count, send, factors, ops):
    vmem, anywhere = pl.BlockSpec(memory_space=pltpu.VMEM), pl.BlockSpec(memory_space=pl.ANY)
    return pl.pallas_call(
        upward_kernel,
        out_shape=(
            jax.ShapeDtypeStruct((ROWS, NODES), BF),
            pltpu.VMEM((PEERS, MSG, LANES), BF),
            pltpu.VMEM((4, NODES, LANES), BF),
            pltpu.VMEM((4, NODES, LANES), BF),
            pltpu.VMEM((2, NODES, LANES), BF),
        ),
        in_specs=[anywhere] * 8,
        out_specs=(vmem,) * 5,
        scratch_shapes=[
            pltpu.VMEM((1, 4), jnp.int32),
            pltpu.VMEM((256, NODES), BF),
            pltpu.VMEM((1, 4, SEG), jnp.int32),
            pltpu.VMEM((1, 4, SEG), jnp.int32),
            pltpu.VMEM((GHOST, SEG), jnp.int32),
            pltpu.VMEM((4 * LANES, 2 * LANES), BF),
            pltpu.VMEM((2 * NODES, NODES), BF),
            pltpu.SemaphoreType.DMA((7,)),
            pltpu.SemaphoreType.DMA((3,)),
        ],
        compiler_params=pltpu.CompilerParams(vmem_limit_bytes=VMEM),
        cost_estimate=pl.CostEstimate(flops=2 * 256 * 512 * 512, bytes_accessed=5 << 20, transcendentals=0),
        name="upward",
    )(count, leaves, target, source, send, *factors, ops)


def pick_kernel(got_ref, out_ref):
    parents = jnp.concatenate([got_ref[j, 0:ROWS, :] for j in range(PEERS)], axis=0)
    send = jnp.concatenate([got_ref[0, ROWS : ROWS + 8, :].astype(F32), got_ref[4, ROWS : ROWS + 8, :].astype(F32) + SEG], axis=0)
    send = send.astype(jnp.int32)
    send = jnp.where(lax.axis_index("c") == 0, send, pltpu.roll(send, LANES - 1, 1))
    at = iota((16, 2 * SEG), 1)
    step = 16
    for first in range(0, CHIPS, step):
        lhs = jnp.concatenate([onehot(send[:, 2 * d : 2 * d + 1] == at) for d in range(first, first + step)], axis=0)
        out_ref[first * 16 : (first + step) * 16, :] = dot(lhs, parents).astype(BF)


def pick(got):
    vmem = pl.BlockSpec(memory_space=pltpu.VMEM)
    return pl.pallas_call(
        pick_kernel,
        out_shape=jax.ShapeDtypeStruct((CHIPS * 16, LANES), BF),
        in_specs=[vmem],
        out_specs=vmem,
        compiler_params=pltpu.CompilerParams(vmem_limit_bytes=SMALL_VMEM),
        cost_estimate=pl.CostEstimate(flops=PLAN_FLOPS, bytes_accessed=1 << 19, transcendentals=0),
        name="pick",
    )(got)


def plan_kernel(got_ref, side_ref, across_ref, out_ref, first_ref, second_ref):
    sub, core = lax.axis_index("x"), lax.axis_index("c")
    groups = []
    for x in (sub, sub + 1 + 2 * core, sub + 3 + 2 * core, sub + 2):
        info = got_ref[core * 4 + (x & 3), ROWS + 8 : MSG, :].astype(F32)
        groups.append(((info[0:4, :] - 1.0) * BASE + info[4:8, :]).astype(jnp.int32))
    first, last = groups[3][0:2, :], groups[3][2:4, :]
    here, there = jnp.where(core == 0, first, last), jnp.where(core == 0, last, first)
    at = 0
    for source in (groups[0], groups[1], here, groups[2], there):
        rows = source.shape[0]
        ghost = source - SEG
        out_ref[at : at + rows, :] = jnp.where(source < SEG, jnp.where(source < 0, -1, source + 256), ghost & 255)
        out_ref[16 + at : 16 + at + rows, :] = jnp.where(source < SEG, 0, ghost >> 8)
        at += rows
    first_ref[...] = side_ref[0:3]
    second_ref[0:1] = side_ref[3:4]
    second_ref[1:3] = across_ref[...]


def plan(got, side, across):
    vmem = pl.BlockSpec(memory_space=pltpu.VMEM)
    return pl.pallas_call(
        plan_kernel,
        out_shape=(jax.ShapeDtypeStruct((32, SEG), jnp.int32),) + (jax.ShapeDtypeStruct((3, NODES, LANES), BF),) * 2,
        in_specs=[vmem] * 3,
        out_specs=(vmem,) * 3,
        compiler_params=pltpu.CompilerParams(vmem_limit_bytes=SMALL_VMEM),
        cost_estimate=pl.CostEstimate(flops=PLAN_FLOPS, bytes_accessed=5 << 20, transcendentals=0),
        name="plan",
    )(got, side, across)


def local_kernel(got_ref, ghosts_ref, plan_ref, own_ref, side_ref, across_ref, first_ref, second_ref, out_ref, rows_ref, rhs_ref, x_ref):
    core = lax.axis_index("c")
    row = iota((WIDTH, SEG), 0)
    for k in range(16):
        rows_ref[:, k * SEG : (k + 1) * SEG] = onehot(plan_ref[k : k + 1, :] == row)
    own = jnp.concatenate([got_ref[core * 4 + j, 0:ROWS, :] for j in range(4)], axis=0).astype(F32).T
    rhs_ref[0:LANES, 256:WIDTH] = own.astype(BF)
    rhs_ref[LANES:512, 256:WIDTH] = jnp.zeros((512 - LANES, SEG), BF)
    for b in range(4):
        rhs_ref[b * LANES : (b + 1) * LANES, 0:256] = ghosts_ref[b * 256 : (b + 1) * 256, :].astype(F32).T.astype(BF)
    total = jnp.zeros((SEG, NODES), F32)
    for k in range(0, 16, 2):
        both = dot(rhs_ref[...], rows_ref[:, k * SEG : (k + 2) * SEG])
        for i in range(2):
            block = plan_ref[16 + k + i : 17 + k + i, :]
            part = both[:, i * SEG : (i + 1) * SEG]
            kept = jnp.where(block == 0, part[0:LANES, :], 0.0)
            for b in range(1, 4):
                kept = jnp.where(block == b, part[b * LANES : (b + 1) * LANES, :], kept)
            x_ref[(k + i) * LANES : (k + i + 1) * LANES, :] = kept.astype(BF)
    held = ((own_ref, 4), (side_ref, 4), (across_ref, 2), (first_ref, 3), (second_ref, 3))
    refs = [ref.at[k] for ref, count in held for k in range(count)]
    for k in range(0, 16, 2):
        pair = jnp.concatenate([refs[k][...], refs[k + 1][...]], axis=1)
        total = total + lax.dot_general(x_ref[k * LANES : (k + 2) * LANES, :], pair, (((0,), (1,)), ((), ())), preferred_element_type=F32)
    out_ref[...] = total.astype(BF)


def local_sums(got, ghosts, columns, *ops):
    vmem = pl.BlockSpec(memory_space=pltpu.VMEM)
    return pl.pallas_call(
        local_kernel,
        out_shape=jax.ShapeDtypeStruct((SEG, NODES), BF),
        in_specs=[vmem] * 8,
        out_specs=vmem,
        scratch_shapes=[
            pltpu.VMEM((WIDTH, 16 * SEG), BF),
            pltpu.VMEM((512, WIDTH), BF),
            pltpu.VMEM((16 * LANES, SEG), BF),
        ],
        compiler_params=pltpu.CompilerParams(vmem_limit_bytes=SMALL_VMEM),
        cost_estimate=pl.CostEstimate(flops=2 * 4096 * 512 * 256, bytes_accessed=5 << 20, transcendentals=0),
        name="local_sums",
    )(got, ghosts, columns, *ops)


def body(factors, leaves, m2l_ops, send_index, pair_target, pair_source, pair_count):
    send = jnp.transpose(send_index, (0, 2, 1)).reshape(GHOST, SEG)
    parents, message, own, side, across = upward(leaves, pair_target, pair_source, pair_count, send, factors, m2l_ops)
    got = lax.all_to_all(message, ("c", "x"), 0, 0, tiled=True)
    steps = [(c * SUBS + i, c * SUBS + (i + 3 + 2 * c) % SUBS) for c in range(2) for i in range(SUBS)]
    side = lax.ppermute(side, ("c", "x"), steps)
    across = lax.ppermute(across, "x", [(i, (i + 2) % SUBS) for i in range(SUBS)])
    ghosts = lax.all_to_all(pick(got), ("y", "z"), 0, 0, tiled=True)
    columns, first, second = plan(got, side, across)
    first = lax.ppermute(first, "c", [(0, 1), (1, 0)])
    second = lax.ppermute(second, "c", [(0, 1), (1, 0)])
    sums = local_sums(got, ghosts, columns, own, side, across, first, second)
    parts = lax.all_to_all(sums, "x", 0, 0, tiled=True)
    local = jnp.sum(parts.reshape(SUBS, ROWS, NODES).astype(F32), axis=0)
    return (parents, local)


def solution(mesh):
    four = Mesh(mesh.devices.reshape(8, 8, 2, SUBS), ("y", "z", "c", "x"))
    slab = ("y", "z", "c")
    every = slab + ("x",)
    in_specs = (
        P(every, None),
        P("x", None, None),
        P(slab, None, None),
        P(slab, "x", None),
        P(slab, "x", None),
        P(slab, "x"),
    )
    out_specs = (P(every, None), P(every, None))
    factors = upward_factors()
    return jax.shard_map(
        lambda *args: body([jnp.asarray(factor) for factor in factors], *args), mesh=four, in_specs=in_specs, out_specs=out_specs, check_vma=False
    )
```

```python
import functools
import math

import jax
import jax.numpy as jnp
import numpy as np
from jax import lax
from jax.experimental import pallas as pl
from jax.experimental.pallas import tpu as pltpu
from jax.sharding import Mesh, PartitionSpec as P

ORDER = 8
NODES = 512
SEG = 128
GHOST = 8
TABLE = 1152
BASE = 32
CHIPS = 64
SUBS = 4
PEERS = 8
ROWS = 32
MSG = 48
EIGHTH = 64
LANES = 128
WIDTH = 640
PLAN_FLOPS = 1 << 34
VMEM = 60 << 20
SMALL_VMEM = 16 << 20
BF = jnp.bfloat16
F32 = jnp.float32


def one_side(side):
    counter = np.arange(ORDER, dtype=np.float32)
    angles = (np.float32(2.0) * counter + np.float32(1.0)) * np.float32(math.pi) / np.float32(2.0 * ORDER)
    nodes = np.cos(angles)
    degree = np.arange(1, ORDER, dtype=np.float32)
    parent_poly = np.cos(degree[:, None] * angles[None, :])
    child_pts = (nodes + np.float32(2.0 * side - 1.0)) / np.float32(2.0)
    child_poly = np.cos(degree[:, None] * np.arccos(child_pts)[None, :])
    summed = np.sum(parent_poly[:, :, None] * child_poly[:, None, :], axis=0)
    return (np.float32(1.0 / ORDER) + np.float32(2.0 / ORDER) * summed).astype(np.float32)


def upward_factors():
    sides = [one_side(0), one_side(1)]
    inner = [np.kron(np.eye(2), np.kron(sides[i >> 1], sides[i & 1]).T) for i in range(4)]
    outer = [np.kron(side.T, np.eye(EIGHTH)) for side in sides]
    inner = np.concatenate(inner).astype(np.float32)
    high = inner.astype(BF)
    low = (inner - high.astype(np.float32)).astype(BF)
    return np.concatenate([high, low], axis=1), np.concatenate(outer).astype(BF)


def dot(a, b):
    return lax.dot_general(a, b, (((1,), (0,)), ((), ())), preferred_element_type=F32)


def dot_t(a, b):
    return lax.dot_general(a, b, (((1,), (1,)), ((), ())), preferred_element_type=F32)


def iota(shape, axis):
    return lax.broadcasted_iota(jnp.int32, shape, axis)


def onehot(flags):
    return jnp.where(flags, 1.0, 0.0).astype(BF)


def upward_kernel(
    count_hbm, leaves_hbm, target_hbm, source_hbm, send_hbm, inner_hbm, outer_hbm, ops_hbm,
    parents_ref, msg_ref, own_ref, side_ref, across_ref,
    count_ref, leaves_ref, target_ref, source_ref, send_ref, inner_ref, outer_ref, sems, out_sems,
):
    sub, core = lax.axis_index("x"), lax.axis_index("c")
    own, beside, across = [pl.multiple_of((x & 3) * LANES, LANES) for x in (sub, sub + 3 + 2 * core, sub + 2)]
    small = ((count_hbm, count_ref), (target_hbm, target_ref), (source_hbm, source_ref), (send_hbm, send_ref))
    copies = [pltpu.make_async_copy(source, to, sems.at[i]) for i, (source, to) in enumerate(small)]
    copies += [pltpu.make_async_copy(leaves_hbm, leaves_ref, sems.at[4])]
    copies += [pltpu.make_async_copy(inner_hbm, inner_ref, sems.at[5]), pltpu.make_async_copy(outer_hbm, outer_ref, sems.at[6])]
    for copy in copies:
        copy.start()
    into = [
        pltpu.make_async_copy(ops_hbm.at[:, :, pl.ds(beside, LANES)], side_ref, out_sems.at[0]),
        pltpu.make_async_copy(ops_hbm.at[pl.ds(2 * core, 2), :, pl.ds(across, LANES)], across_ref, out_sems.at[1]),
        pltpu.make_async_copy(ops_hbm.at[:, :, pl.ds(own, LANES)], own_ref, out_sems.at[2]),
    ]
    for copy in into:
        copy.start()
    to, at = iota((256, 256), 0), iota((256, 256), 1)
    sort = onehot(at == (to & 31) * 8 + (to >> 5))
    for copy in copies[:4]:
        copy.wait()
    slot = iota((1, SEG), 1)
    row = iota((8, SEG), 0)
    digits, matches = [], []
    for k in range(4):
        live = slot < count_ref[0:1, k : k + 1]
        target = jnp.where(live, target_ref[0, k : k + 1, :], -1)
        source = source_ref[0, k : k + 1, :]
        high = jnp.where(live, (source >> 5) + 1, 0).astype(F32)
        low = jnp.where(live, source & (BASE - 1), 0).astype(F32)
        digits.append(jnp.where(row == k, high, jnp.where(row == 4 + k, low, 0.0)).astype(BF))
        matches.append(onehot(iota((SEG, SEG), 0) == target))
    info = dot_t(jnp.concatenate(digits, axis=1), jnp.concatenate(matches, axis=1))
    tail = jnp.concatenate([send_ref[...].astype(F32), info], axis=0).astype(BF)
    for e in range(PEERS):
        msg_ref[e, ROWS:MSG, :] = tail
    copies[4].wait()
    sorted_leaves = dot(sort, leaves_ref[...]).astype(BF)
    copies[5].wait()
    lhs = []
    for x in range(2):
        for j in range(4):
            parts = [sorted_leaves[(4 * x + i) * ROWS : (4 * x + i + 1) * ROWS, j * LANES : (j + 1) * LANES] for i in range(4)]
            lhs.append(jnp.concatenate(parts, axis=1))
    both = dot(jnp.concatenate(lhs, axis=0), inner_ref[...])
    partial = both[:, 0:LANES] + both[:, LANES:]
    partial = jnp.concatenate([partial[i * ROWS : (i + 1) * ROWS, :] for i in range(8)], axis=1)
    high = partial.astype(BF)
    low = (partial - high.astype(F32)).astype(BF)
    copies[6].wait()
    total = dot(jnp.concatenate([high, low], axis=0), outer_ref[...])
    total = total[0:ROWS, :] + total[ROWS:, :]
    parents = total.astype(BF)
    parents_ref[...] = parents
    for j in range(PEERS):
        msg_ref[j, 0:ROWS, :] = parents[:, (j & 3) * LANES : ((j & 3) + 1) * LANES]
    for copy in into:
        copy.wait()


def upward(leaves, target, source, count, send, factors, ops):
    vmem, anywhere = pl.BlockSpec(memory_space=pltpu.VMEM), pl.BlockSpec(memory_space=pl.ANY)
    return pl.pallas_call(
        upward_kernel,
        out_shape=(
            jax.ShapeDtypeStruct((ROWS, NODES), BF),
            pltpu.VMEM((PEERS, MSG, LANES), BF),
            pltpu.VMEM((4, NODES, LANES), BF),
            pltpu.VMEM((4, NODES, LANES), BF),
            pltpu.VMEM((2, NODES, LANES), BF),
        ),
        in_specs=[anywhere] * 8,
        out_specs=(vmem,) * 5,
        scratch_shapes=[
            pltpu.VMEM((1, 4), jnp.int32),
            pltpu.VMEM((256, NODES), BF),
            pltpu.VMEM((1, 4, SEG), jnp.int32),
            pltpu.VMEM((1, 4, SEG), jnp.int32),
            pltpu.VMEM((GHOST, SEG), jnp.int32),
            pltpu.VMEM((4 * LANES, 2 * LANES), BF),
            pltpu.VMEM((2 * NODES, NODES), BF),
            pltpu.SemaphoreType.DMA((7,)),
            pltpu.SemaphoreType.DMA((3,)),
        ],
        compiler_params=pltpu.CompilerParams(vmem_limit_bytes=VMEM),
        cost_estimate=pl.CostEstimate(flops=2 * 256 * 512 * 512, bytes_accessed=5 << 20, transcendentals=0),
        name="upward",
    )(count, leaves, target, source, send, *factors, ops)


def pick_kernel(got_ref, out_ref):
    parents = jnp.concatenate([got_ref[j, 0:ROWS, :] for j in range(PEERS)], axis=0)
    send = jnp.concatenate([got_ref[0, ROWS : ROWS + 8, :].astype(F32), got_ref[4, ROWS : ROWS + 8, :].astype(F32) + SEG], axis=0)
    send = send.astype(jnp.int32)
    send = jnp.where(lax.axis_index("c") == 0, send, pltpu.roll(send, LANES - 1, 1))
    at = iota((16, 2 * SEG), 1)
    step = 16
    for first in range(0, CHIPS, step):
        lhs = jnp.concatenate([onehot(send[:, 2 * d : 2 * d + 1] == at) for d in range(first, first + step)], axis=0)
        out_ref[first * 16 : (first + step) * 16, :] = dot(lhs, parents).astype(BF)


def pick(got):
    vmem = pl.BlockSpec(memory_space=pltpu.VMEM)
    return pl.pallas_call(
        pick_kernel,
        out_shape=jax.ShapeDtypeStruct((CHIPS * 16, LANES), BF),
        in_specs=[vmem],
        out_specs=vmem,
        compiler_params=pltpu.CompilerParams(vmem_limit_bytes=SMALL_VMEM),
        cost_estimate=pl.CostEstimate(flops=PLAN_FLOPS, bytes_accessed=1 << 19, transcendentals=0),
        name="pick",
    )(got)


def plan_kernel(got_ref, side_ref, across_ref, out_ref, first_ref, second_ref):
    sub, core = lax.axis_index("x"), lax.axis_index("c")
    groups = []
    for x in (sub, sub + 1 + 2 * core, sub + 3 + 2 * core, sub + 2):
        info = got_ref[core * 4 + (x & 3), ROWS + 8 : MSG, :].astype(F32)
        groups.append(((info[0:4, :] - 1.0) * BASE + info[4:8, :]).astype(jnp.int32))
    first, last = groups[3][0:2, :], groups[3][2:4, :]
    here, there = jnp.where(core == 0, first, last), jnp.where(core == 0, last, first)
    at = 0
    for source in (groups[0], groups[1], here, groups[2], there):
        rows = source.shape[0]
        ghost = source - SEG
        out_ref[at : at + rows, :] = jnp.where(source < SEG, jnp.where(source < 0, -1, source + 512), ghost & 511)
        out_ref[16 + at : 16 + at + rows, :] = jnp.where(source < SEG, 0, ghost >> 9)
        at += rows
    first_ref[...] = side_ref[0:3]
    second_ref[0:1] = side_ref[3:4]
    second_ref[1:3] = across_ref[...]


def plan(got, side, across):
    vmem = pl.BlockSpec(memory_space=pltpu.VMEM)
    return pl.pallas_call(
        plan_kernel,
        out_shape=(jax.ShapeDtypeStruct((32, SEG), jnp.int32),) + (jax.ShapeDtypeStruct((3, NODES, LANES), BF),) * 2,
        in_specs=[vmem] * 3,
        out_specs=(vmem,) * 3,
        compiler_params=pltpu.CompilerParams(vmem_limit_bytes=SMALL_VMEM),
        cost_estimate=pl.CostEstimate(flops=PLAN_FLOPS, bytes_accessed=5 << 20, transcendentals=0),
        name="plan",
    )(got, side, across)


def local_kernel(got_ref, ghosts_ref, plan_ref, own_ref, side_ref, across_ref, first_ref, second_ref, out_ref, rows_ref, rhs_ref, x_ref):
    core = lax.axis_index("c")
    row = iota((WIDTH, SEG), 0)
    for k in range(16):
        rows_ref[:, k * SEG : (k + 1) * SEG] = onehot(plan_ref[k : k + 1, :] == row)
    own = jnp.concatenate([got_ref[core * 4 + j, 0:ROWS, :] for j in range(4)], axis=0).astype(F32).T
    rhs_ref[0:LANES, 512:WIDTH] = own.astype(BF)
    rhs_ref[LANES:256, 512:WIDTH] = jnp.zeros((LANES, SEG), BF)
    for b in range(2):
        rhs_ref[b * LANES : (b + 1) * LANES, 0:512] = ghosts_ref[b * 512 : (b + 1) * 512, :].astype(F32).T.astype(BF)
    total = jnp.zeros((SEG, NODES), F32)
    for k in range(0, 16, 2):
        both = dot(rhs_ref[...], rows_ref[:, k * SEG : (k + 2) * SEG])
        for i in range(2):
            block = plan_ref[16 + k + i : 17 + k + i, :]
            part = both[:, i * SEG : (i + 1) * SEG]
            kept = jnp.where(block == 0, part[0:LANES, :], 0.0)
            for b in range(1, 2):
                kept = jnp.where(block == b, part[b * LANES : (b + 1) * LANES, :], kept)
            x_ref[(k + i) * LANES : (k + i + 1) * LANES, :] = kept.astype(BF)
    held = ((own_ref, 4), (side_ref, 4), (across_ref, 2), (first_ref, 3), (second_ref, 3))
    refs = [ref.at[k] for ref, count in held for k in range(count)]
    for k in range(16):
        total = total + lax.dot_general(x_ref[k * LANES : (k + 1) * LANES, :], refs[k][...], (((0,), (1,)), ((), ())), preferred_element_type=F32)
    out_ref[...] = total.astype(BF)


def local_sums(got, ghosts, columns, *ops):
    vmem = pl.BlockSpec(memory_space=pltpu.VMEM)
    return pl.pallas_call(
        local_kernel,
        out_shape=jax.ShapeDtypeStruct((SEG, NODES), BF),
        in_specs=[vmem] * 8,
        out_specs=vmem,
        scratch_shapes=[
            pltpu.VMEM((WIDTH, 16 * SEG), BF),
            pltpu.VMEM((256, WIDTH), BF),
            pltpu.VMEM((16 * LANES, SEG), BF),
        ],
        compiler_params=pltpu.CompilerParams(vmem_limit_bytes=SMALL_VMEM),
        cost_estimate=pl.CostEstimate(flops=2 * 4096 * 512 * 256, bytes_accessed=5 << 20, transcendentals=0),
        name="local_sums",
    )(got, ghosts, columns, *ops)


def body(factors, leaves, m2l_ops, send_index, pair_target, pair_source, pair_count):
    send = jnp.transpose(send_index, (0, 2, 1)).reshape(GHOST, SEG)
    parents, message, own, side, across = upward(leaves, pair_target, pair_source, pair_count, send, factors, m2l_ops)
    got = lax.all_to_all(message, ("c", "x"), 0, 0, tiled=True)
    steps = [(c * SUBS + i, c * SUBS + (i + 3 + 2 * c) % SUBS) for c in range(2) for i in range(SUBS)]
    side = lax.ppermute(side, ("c", "x"), steps)
    across = lax.ppermute(across, "x", [(i, (i + 2) % SUBS) for i in range(SUBS)])
    ghosts = lax.all_to_all(pick(got), ("y", "z"), 0, 0, tiled=True)
    columns, first, second = plan(got, side, across)
    first = lax.ppermute(first, "c", [(0, 1), (1, 0)])
    second = lax.ppermute(second, "c", [(0, 1), (1, 0)])
    sums = local_sums(got, ghosts, columns, own, side, across, first, second)
    parts = lax.all_to_all(sums, "x", 0, 0, tiled=True)
    local = jnp.sum(parts.reshape(SUBS, ROWS, NODES).astype(F32), axis=0)
    return (parents, local)


def solution(mesh):
    four = Mesh(mesh.devices.reshape(8, 8, 2, SUBS), ("y", "z", "c", "x"))
    slab = ("y", "z", "c")
    every = slab + ("x",)
    in_specs = (
        P(every, None),
        P("x", None, None),
        P(slab, None, None),
        P(slab, "x", None),
        P(slab, "x", None),
        P(slab, "x"),
    )
    out_specs = (P(every, None), P(every, None))
    factors = upward_factors()
    return jax.shard_map(
        lambda *args: body([jnp.asarray(factor) for factor in factors], *args), mesh=four, in_specs=in_specs, out_specs=out_specs, check_vma=False
    )
```

```python
import functools
import math

import jax
import jax.numpy as jnp
import numpy as np
from jax import lax
from jax.experimental import pallas as pl
from jax.experimental.pallas import tpu as pltpu
from jax.sharding import Mesh, PartitionSpec as P

ORDER = 8
NODES = 512
SEG = 128
GHOST = 8
TABLE = 1152
BASE = 32
CHIPS = 64
SUBS = 4
PEERS = 8
ROWS = 32
MSG = 48
EIGHTH = 64
LANES = 128
WIDTH = 640
PLAN_FLOPS = 1 << 34
VMEM = 60 << 20
SMALL_VMEM = 16 << 20
BF = jnp.bfloat16
F32 = jnp.float32


def one_side(side):
    counter = np.arange(ORDER, dtype=np.float32)
    angles = (np.float32(2.0) * counter + np.float32(1.0)) * np.float32(math.pi) / np.float32(2.0 * ORDER)
    nodes = np.cos(angles)
    degree = np.arange(1, ORDER, dtype=np.float32)
    parent_poly = np.cos(degree[:, None] * angles[None, :])
    child_pts = (nodes + np.float32(2.0 * side - 1.0)) / np.float32(2.0)
    child_poly = np.cos(degree[:, None] * np.arccos(child_pts)[None, :])
    summed = np.sum(parent_poly[:, :, None] * child_poly[:, None, :], axis=0)
    return (np.float32(1.0 / ORDER) + np.float32(2.0 / ORDER) * summed).astype(np.float32)


def upward_factors():
    sides = [one_side(0), one_side(1)]
    inner = [np.kron(np.eye(2), np.kron(sides[i >> 1], sides[i & 1]).T) for i in range(4)]
    outer = [np.kron(side.T, np.eye(EIGHTH)) for side in sides]
    inner = np.concatenate(inner).astype(np.float32)
    high = inner.astype(BF)
    low = (inner - high.astype(np.float32)).astype(BF)
    return np.concatenate([high, low], axis=1), np.concatenate(outer).astype(BF)


def dot(a, b):
    return lax.dot_general(a, b, (((1,), (0,)), ((), ())), preferred_element_type=F32)


def dot_t(a, b):
    return lax.dot_general(a, b, (((1,), (1,)), ((), ())), preferred_element_type=F32)


def iota(shape, axis):
    return lax.broadcasted_iota(jnp.int32, shape, axis)


def onehot(flags):
    return jnp.where(flags, 1.0, 0.0).astype(BF)


def upward_kernel(
    count_hbm, leaves_hbm, target_hbm, source_hbm, send_hbm, inner_hbm, outer_hbm, ops_hbm,
    parents_ref, msg_ref, own_ref, side_ref, across_ref,
    count_ref, leaves_ref, target_ref, source_ref, send_ref, inner_ref, outer_ref, sems, out_sems,
):
    sub, core = lax.axis_index("x"), lax.axis_index("c")
    own, beside, across = [pl.multiple_of((x & 3) * LANES, LANES) for x in (sub, sub + 3 + 2 * core, sub + 2)]
    small = ((count_hbm, count_ref), (target_hbm, target_ref), (source_hbm, source_ref), (send_hbm, send_ref))
    copies = [pltpu.make_async_copy(source, to, sems.at[i]) for i, (source, to) in enumerate(small)]
    copies += [pltpu.make_async_copy(leaves_hbm, leaves_ref, sems.at[4])]
    copies += [pltpu.make_async_copy(inner_hbm, inner_ref, sems.at[5]), pltpu.make_async_copy(outer_hbm, outer_ref, sems.at[6])]
    for copy in copies:
        copy.start()
    into = [
        pltpu.make_async_copy(ops_hbm.at[:, :, pl.ds(beside, LANES)], side_ref, out_sems.at[0]),
        pltpu.make_async_copy(ops_hbm.at[pl.ds(2 * core, 2), :, pl.ds(across, LANES)], across_ref, out_sems.at[1]),
        pltpu.make_async_copy(ops_hbm.at[:, :, pl.ds(own, LANES)], own_ref, out_sems.at[2]),
    ]
    for copy in into:
        copy.start()
    to, at = iota((256, 256), 0), iota((256, 256), 1)
    sort = onehot(at == (to & 31) * 8 + (to >> 5))
    for copy in copies[:4]:
        copy.wait()
    slot = iota((1, SEG), 1)
    row = iota((8, SEG), 0)
    digits, matches = [], []
    for k in range(4):
        live = slot < count_ref[0:1, k : k + 1]
        target = jnp.where(live, target_ref[0, k : k + 1, :], -1)
        source = source_ref[0, k : k + 1, :]
        high = jnp.where(live, (source >> 5) + 1, 0).astype(F32)
        low = jnp.where(live, source & (BASE - 1), 0).astype(F32)
        digits.append(jnp.where(row == k, high, jnp.where(row == 4 + k, low, 0.0)).astype(BF))
        matches.append(onehot(iota((SEG, SEG), 0) == target))
    info = dot_t(jnp.concatenate(digits, axis=1), jnp.concatenate(matches, axis=1))
    tail = jnp.concatenate([send_ref[...].astype(F32), info], axis=0).astype(BF)
    for e in range(PEERS):
        msg_ref[e, ROWS:MSG, :] = tail
    copies[4].wait()
    sorted_leaves = dot(sort, leaves_ref[...]).astype(BF)
    copies[5].wait()
    lhs = []
    for x in range(2):
        for j in range(4):
            parts = [sorted_leaves[(4 * x + i) * ROWS : (4 * x + i + 1) * ROWS, j * LANES : (j + 1) * LANES] for i in range(4)]
            lhs.append(jnp.concatenate(parts, axis=1))
    both = dot(jnp.concatenate(lhs, axis=0), inner_ref[...])
    partial = both[:, 0:LANES] + both[:, LANES:]
    partial = jnp.concatenate([partial[i * ROWS : (i + 1) * ROWS, :] for i in range(8)], axis=1)
    high = partial.astype(BF)
    low = (partial - high.astype(F32)).astype(BF)
    copies[6].wait()
    total = dot(jnp.concatenate([high, low], axis=0), outer_ref[...])
    total = total[0:ROWS, :] + total[ROWS:, :]
    parents = total.astype(BF)
    parents_ref[...] = parents
    for j in range(PEERS):
        msg_ref[j, 0:ROWS, :] = parents[:, (j & 3) * LANES : ((j & 3) + 1) * LANES]
    for copy in into:
        copy.wait()


def upward(leaves, target, source, count, send, factors, ops):
    vmem, anywhere = pl.BlockSpec(memory_space=pltpu.VMEM), pl.BlockSpec(memory_space=pl.ANY)
    return pl.pallas_call(
        upward_kernel,
        out_shape=(
            jax.ShapeDtypeStruct((ROWS, NODES), BF),
            pltpu.VMEM((PEERS, MSG, LANES), BF),
            pltpu.VMEM((4, NODES, LANES), BF),
            pltpu.VMEM((4, NODES, LANES), BF),
            pltpu.VMEM((2, NODES, LANES), BF),
        ),
        in_specs=[anywhere] * 8,
        out_specs=(vmem,) * 5,
        scratch_shapes=[
            pltpu.VMEM((1, 4), jnp.int32),
            pltpu.VMEM((256, NODES), BF),
            pltpu.VMEM((1, 4, SEG), jnp.int32),
            pltpu.VMEM((1, 4, SEG), jnp.int32),
            pltpu.VMEM((GHOST, SEG), jnp.int32),
            pltpu.VMEM((4 * LANES, 2 * LANES), BF),
            pltpu.VMEM((2 * NODES, NODES), BF),
            pltpu.SemaphoreType.DMA((7,)),
            pltpu.SemaphoreType.DMA((3,)),
        ],
        compiler_params=pltpu.CompilerParams(vmem_limit_bytes=VMEM),
        cost_estimate=pl.CostEstimate(flops=2 * 256 * 512 * 512, bytes_accessed=5 << 20, transcendentals=0),
        name="upward",
    )(count, leaves, target, source, send, *factors, ops)


def pick_kernel(got_ref, out_ref):
    parents = jnp.concatenate([got_ref[j, 0:ROWS, :] for j in range(PEERS)], axis=0)
    send = jnp.concatenate([got_ref[0, ROWS : ROWS + 8, :].astype(F32), got_ref[4, ROWS : ROWS + 8, :].astype(F32) + SEG], axis=0)
    send = send.astype(jnp.int32)
    send = jnp.where(lax.axis_index("c") == 0, send, pltpu.roll(send, LANES - 1, 1))
    at = iota((16, 2 * SEG), 1)
    step = 16
    for first in range(0, CHIPS, step):
        lhs = jnp.concatenate([onehot(send[:, 2 * d : 2 * d + 1] == at) for d in range(first, first + step)], axis=0)
        out_ref[first * 16 : (first + step) * 16, :] = dot(lhs, parents).astype(BF)


def pick(got):
    vmem = pl.BlockSpec(memory_space=pltpu.VMEM)
    return pl.pallas_call(
        pick_kernel,
        out_shape=jax.ShapeDtypeStruct((CHIPS * 16, LANES), BF),
        in_specs=[vmem],
        out_specs=vmem,
        compiler_params=pltpu.CompilerParams(vmem_limit_bytes=SMALL_VMEM),
        cost_estimate=pl.CostEstimate(flops=PLAN_FLOPS, bytes_accessed=1 << 19, transcendentals=0),
        name="pick",
    )(got)


def plan_kernel(got_ref, side_ref, across_ref, out_ref, first_ref, second_ref):
    sub, core = lax.axis_index("x"), lax.axis_index("c")
    groups = []
    for x in (sub, sub + 1 + 2 * core, sub + 3 + 2 * core, sub + 2):
        info = got_ref[core * 4 + (x & 3), ROWS + 8 : MSG, :].astype(F32)
        groups.append(((info[0:4, :] - 1.0) * BASE + info[4:8, :]).astype(jnp.int32))
    first, last = groups[3][0:2, :], groups[3][2:4, :]
    here, there = jnp.where(core == 0, first, last), jnp.where(core == 0, last, first)
    at = 0
    for source in (groups[0], groups[1], here, groups[2], there):
        rows = source.shape[0]
        ghost = source - SEG
        out_ref[at : at + rows, :] = jnp.where(source < SEG, jnp.where(source < 0, -1, source + 512), ghost & 511)
        out_ref[16 + at : 16 + at + rows, :] = jnp.where(source < SEG, 0, ghost >> 9)
        at += rows
    first_ref[...] = side_ref[0:3]
    second_ref[0:1] = side_ref[3:4]
    second_ref[1:3] = across_ref[...]


def plan(got, side, across):
    vmem = pl.BlockSpec(memory_space=pltpu.VMEM)
    return pl.pallas_call(
        plan_kernel,
        out_shape=(jax.ShapeDtypeStruct((32, SEG), jnp.int32),) + (jax.ShapeDtypeStruct((3, NODES, LANES), BF),) * 2,
        in_specs=[vmem] * 3,
        out_specs=(vmem,) * 3,
        compiler_params=pltpu.CompilerParams(vmem_limit_bytes=SMALL_VMEM),
        cost_estimate=pl.CostEstimate(flops=PLAN_FLOPS, bytes_accessed=5 << 20, transcendentals=0),
        name="plan",
    )(got, side, across)


def local_kernel(got_ref, ghosts_ref, plan_ref, own_ref, side_ref, across_ref, first_ref, second_ref, out_ref, rows_ref, rhs_ref, x_ref):
    core = lax.axis_index("c")
    row = iota((WIDTH, SEG), 0).astype(jnp.int16)
    place = plan_ref[0:16, :].astype(jnp.int16)
    one, zero = jnp.ones((WIDTH, SEG), BF), jnp.zeros((WIDTH, SEG), BF)
    for k in range(16):
        rows_ref[:, k * SEG : (k + 1) * SEG] = jnp.where(place[k : k + 1, :] == row, one, zero)
    own = jnp.concatenate([got_ref[core * 4 + j, 0:ROWS, :] for j in range(4)], axis=0).astype(F32).T
    rhs_ref[0:LANES, 512:WIDTH] = own.astype(BF)
    rhs_ref[LANES:256, 512:WIDTH] = jnp.zeros((LANES, SEG), BF)
    for b in range(2):
        rhs_ref[b * LANES : (b + 1) * LANES, 0:512] = ghosts_ref[b * 512 : (b + 1) * 512, :].astype(F32).T.astype(BF)
    total = jnp.zeros((SEG, NODES), F32)
    for k in range(0, 16, 2):
        both = dot(rhs_ref[...], rows_ref[:, k * SEG : (k + 2) * SEG])
        for i in range(2):
            block = plan_ref[16 + k + i : 17 + k + i, :]
            part = both[:, i * SEG : (i + 1) * SEG]
            kept = jnp.where(block == 0, part[0:LANES, :], 0.0)
            for b in range(1, 2):
                kept = jnp.where(block == b, part[b * LANES : (b + 1) * LANES, :], kept)
            x_ref[(k + i) * LANES : (k + i + 1) * LANES, :] = kept.astype(BF)
    held = ((own_ref, 4), (side_ref, 4), (across_ref, 2), (first_ref, 3), (second_ref, 3))
    refs = [ref.at[k] for ref, count in held for k in range(count)]
    for k in range(16):
        total = total + lax.dot_general(x_ref[k * LANES : (k + 1) * LANES, :], refs[k][...], (((0,), (1,)), ((), ())), preferred_element_type=F32)
    out_ref[...] = total.astype(BF)


def local_sums(got, ghosts, columns, *ops):
    vmem = pl.BlockSpec(memory_space=pltpu.VMEM)
    return pl.pallas_call(
        local_kernel,
        out_shape=jax.ShapeDtypeStruct((SEG, NODES), BF),
        in_specs=[vmem] * 8,
        out_specs=vmem,
        scratch_shapes=[
            pltpu.VMEM((WIDTH, 16 * SEG), BF),
            pltpu.VMEM((256, WIDTH), BF),
            pltpu.VMEM((16 * LANES, SEG), BF),
        ],
        compiler_params=pltpu.CompilerParams(vmem_limit_bytes=SMALL_VMEM),
        cost_estimate=pl.CostEstimate(flops=2 * 4096 * 512 * 256, bytes_accessed=5 << 20, transcendentals=0),
        name="local_sums",
    )(got, ghosts, columns, *ops)


def body(factors, leaves, m2l_ops, send_index, pair_target, pair_source, pair_count):
    send = jnp.transpose(send_index, (0, 2, 1)).reshape(GHOST, SEG)
    parents, message, own, side, across = upward(leaves, pair_target, pair_source, pair_count, send, factors, m2l_ops)
    got = lax.all_to_all(message, ("c", "x"), 0, 0, tiled=True)
    steps = [(c * SUBS + i, c * SUBS + (i + 3 + 2 * c) % SUBS) for c in range(2) for i in range(SUBS)]
    side = lax.ppermute(side, ("c", "x"), steps)
    across = lax.ppermute(across, "x", [(i, (i + 2) % SUBS) for i in range(SUBS)])
    ghosts = lax.all_to_all(pick(got), ("y", "z"), 0, 0, tiled=True)
    columns, first, second = plan(got, side, across)
    first = lax.ppermute(first, "c", [(0, 1), (1, 0)])
    second = lax.ppermute(second, "c", [(0, 1), (1, 0)])
    sums = local_sums(got, ghosts, columns, own, side, across, first, second)
    parts = lax.all_to_all(sums, "x", 0, 0, tiled=True)
    local = jnp.sum(parts.reshape(SUBS, ROWS, NODES).astype(F32), axis=0)
    return (parents, local)


def solution(mesh):
    four = Mesh(mesh.devices.reshape(8, 8, 2, SUBS), ("y", "z", "c", "x"))
    slab = ("y", "z", "c")
    every = slab + ("x",)
    in_specs = (
        P(every, None),
        P("x", None, None),
        P(slab, None, None),
        P(slab, "x", None),
        P(slab, "x", None),
        P(slab, "x"),
    )
    out_specs = (P(every, None), P(every, None))
    factors = upward_factors()
    return jax.shard_map(
        lambda *args: body([jnp.asarray(factor) for factor in factors], *args), mesh=four, in_specs=in_specs, out_specs=out_specs, check_vma=False
    )
```
